256 devices in a mesh: gy: 8 (over y, x_hi), gx: 32 (over z, x_lo, core).
Axes of the slice: x: 4 (x_hi: 2, x_lo: 2; x = x_hi * 2 + x_lo), y: 4, z: 8, core: 2. Of those that a mesh axis runs over, the one named last changes fastest.
Arguments:
- current: float32 [256, 1024, 128], P('gy', 'gx'), may hold values from 0.25 to 4
- recorded: float32 [4, 256, 1024, 128], P(None, 'gy', 'gx'), may hold values from 0.25 to 4
- psf_depth: float32 [4, 31], replicated, may hold values from 0.02 to 1
- psf_rows: float32 [4, 31], replicated, may hold values from 0.02 to 1
- psf_cols: float32 [4, 31], replicated, may hold values from 0.02 to 1
Outputs:
- updated: float32 [256, 1024, 128], P('gy', 'gx')
The draws below stay inside these ranges and needn't reach their ends.
All inputs are finite; a program needn't handle non-finite values.
Results may differ from the reference program's by a relative error of at most 0.0001.
Values sent between devices are 32-bit elements; how exact they have to be, the bound alone decides.
A program may use at most 192 MiB of HBM per device.

```python
import math
import jax
import jax.numpy as jnp
from jax import lax

DEPTH = 128
VIEWS = 4
TAPS = 31
ROWS = 256
COLS = 1024


def level_of(own_key, dims, shards, least, top_value):
    level, own = 1.0, jax.random.fold_in(own_key, 6)
    for position, blocks in shards:
        heights = jnp.exp(jax.random.uniform(jax.random.fold_in(own, position), (blocks,), jnp.float32, least / len(shards), top_value / len(shards)))
        level = level * jnp.repeat(heights, dims[position] // blocks).reshape([-1 if axis == position else 1 for axis in range(len(dims))])
    return level


def setup_inputs(seed: int = 0) -> dict:
    key_list = jax.random.split(jax.random.key(seed), 6)
    return {
        "current": jnp.clip(jnp.exp(math.log(4.0) - 2.7725887 * jax.random.uniform(key_list[0], (ROWS, COLS, DEPTH), jnp.float32) ** level_of(key_list[0], (ROWS, COLS, DEPTH), ((0, 8), (1, 32)), -0.2, 0.2)), 0.25, 4.0),
        "recorded": jnp.clip(jnp.exp(math.log(4.0) - 2.7725887 * jax.random.uniform(key_list[1], (VIEWS, ROWS, COLS, DEPTH), jnp.float32) ** level_of(key_list[1], (VIEWS, ROWS, COLS, DEPTH), ((1, 8), (2, 32)), -0.2, 0.2)), 0.25, 4.0),
        "psf_depth": jnp.clip(jnp.exp(jax.random.uniform(key_list[2], (VIEWS, TAPS), jnp.float32, math.log(0.02), math.log(1.0))), 0.02, 1.0),
        "psf_rows": jnp.clip(jnp.exp(jax.random.uniform(key_list[3], (VIEWS, TAPS), jnp.float32, math.log(0.02), math.log(1.0))), 0.02, 1.0),
        "psf_cols": jnp.clip(jnp.exp(jax.random.uniform(key_list[4], (VIEWS, TAPS), jnp.float32, math.log(0.02), math.log(1.0))), 0.02, 1.0),
    }


def normalized(kernel):
    return kernel / jnp.sum(kernel, axis=-1, keepdims=True)


def taps_valid(padded, weights, dimension, length):
    result = None
    for k in range(weights.shape[0]):
        window_part = lax.slice_in_dim(padded, k, k + length, axis=dimension)
        term = weights[k] * window_part
        result = term if result is None else result + term
    return result


def convolve(volume, weights, dimension):
    radius = weights.shape[0] // 2
    padding = [(0, 0)] * volume.ndim
    padding[dimension] = (radius, radius)
    return taps_valid(jnp.pad(volume, padding), weights, dimension, volume.shape[dimension])


def reference(current, recorded, psf_depth, psf_rows, psf_cols):
    depth_taps = normalized(psf_depth)
    row_taps = normalized(psf_rows)
    col_taps = normalized(psf_cols)

    def one_view(carry, items):
        image, depth_w, row_w, col_w = items
        blurred = convolve(convolve(convolve(current, depth_w, 2), row_w, 0), col_w, 1)
        quotient = image / blurred
        backed = convolve(convolve(convolve(quotient, col_w[::-1], 1), row_w[::-1], 0), depth_w[::-1], 2)
        return carry + backed, None

    summed, unused = lax.scan(one_view, jnp.zeros_like(current), (recorded, depth_taps, row_taps, col_taps))
    return current * (summed / VIEWS)
```

```python
import functools

import jax
import jax.numpy as jnp
from jax import lax
from jax.experimental import pallas as pl
from jax.experimental.pallas import tpu as pltpu
from jax.sharding import PartitionSpec as P

F32 = jnp.float32
BF16 = jnp.bfloat16
TAPS = 31
RAD = 15
VIEWS = 4
B = 32
H = 16
ROWS = B + 2 * RAD
COLS = B + 2 * H
Z = 128


def split(x):
    hi = x.astype(BF16)
    return hi, (x - hi.astype(F32)).astype(BF16)


def triple_rows(x):
    hi, lo = split(x)
    return jnp.concatenate([hi, lo, hi], axis=0)


def triple_lanes(x):
    hi, lo = split(x)
    return jnp.concatenate([hi, lo, hi], axis=1)


def dot(a, b):
    return jnp.dot(a, b, preferred_element_type=F32)


def tap_sum(ref, v):
    total = ref[v, 0]
    for t in range(1, TAPS):
        total = total + ref[v, t]
    return total


def kernel(ny, nx, cur, rec, kz, ky, kx, out, u, xb, yb, rv, p, ry, rxp, rxo, rd, rpc,
           tf, tb, wf, wb, local_sem, send_sem, recv_sem):
    i = lax.axis_index("gy")
    j = lax.axis_index("gx")
    side = lax.rem(j, 2)
    up = lax.rem(i + ny - 1, ny)
    down = lax.rem(i + 1, ny)
    away = lax.rem(j + nx - 1 + 2 * side, nx)
    mate = j + 1 - 2 * side

    def col(x):
        return pl.ds(pl.multiple_of(x, H), H)

    own_away = H * side
    own_mate = H * (1 - side)
    halo_away = 48 * side
    halo_mate = 48 * (1 - side)

    load_rec = pltpu.make_async_copy(rec, rv, local_sem.at[0])
    load_cur = pltpu.make_async_copy(cur, u.at[pl.ds(RAD, B), pl.ds(H, B), :], local_sem.at[1])
    load_cur.start()
    load_rec.start()

    barrier = pltpu.get_barrier_semaphore()
    peers = [(up, j), (down, j), (i, away), (i, mate), (up, away), (down, away)]
    for peer in peers:
        pl.semaphore_signal(barrier, inc=1, device_id=peer, device_id_type=pl.DeviceIdType.MESH)
    pl.semaphore_wait(barrier, len(peers))

    def remote(k, src, dst, peer):
        return pltpu.make_async_remote_copy(
            src_ref=src, dst_ref=dst, send_sem=send_sem.at[k], recv_sem=recv_sem.at[k],
            device_id=peer, device_id_type=pl.DeviceIdType.MESH)

    top = pl.ds(0, RAD)
    bottom = pl.ds(RAD + B, RAD)
    mid = pl.ds(RAD, B)
    first = pl.ds(0, RAD)
    last = pl.ds(B - RAD, RAD)

    up_mate = remote(0, cur.at[first, col(own_mate), :], u.at[bottom, col(H + own_mate), :], (up, j))
    down_mate = remote(1, cur.at[last, col(own_mate), :], u.at[top, col(H + own_mate), :], (down, j))
    up_away = remote(2, cur.at[first, col(own_away), :], u.at[bottom, col(H + own_away), :], (up, j))
    down_away = remote(3, cur.at[last, col(own_away), :], u.at[top, col(H + own_away), :], (down, j))
    side_away = remote(4, cur.at[:, col(own_away), :], u.at[mid, col(48 - halo_away), :], (i, away))
    side_mate = remote(5, cur.at[:, col(own_mate), :], u.at[mid, col(48 - halo_mate), :], (i, mate))
    diag_up = remote(6, cur.at[first, col(own_away), :], u.at[bottom, col(48 - halo_away), :], (up, away))
    diag_down = remote(7, cur.at[last, col(own_away), :], u.at[top, col(48 - halo_away), :], (down, away))
    pass_top = remote(8, u.at[top, col(H + own_mate), :], u.at[top, col(48 - halo_mate), :], (i, mate))
    pass_bottom = remote(9, u.at[bottom, col(H + own_mate), :], u.at[bottom, col(48 - halo_mate), :], (i, mate))
    for c in (side_mate, side_away, up_mate, down_mate, up_away, down_away, diag_up, diag_down):
        c.start()

    row_id = lax.broadcasted_iota(jnp.int32, (B, Z), 0)
    lane_id = lax.broadcasted_iota(jnp.int32, (B, Z), 1)
    low = jnp.where(j == 0, H, 0)
    high = jnp.where(j == nx - 1, H + B, COLS)
    inside = (lane_id >= low) & (lane_id < high)
    parts = []
    for v in range(VIEWS):
        band = jnp.zeros((B, Z), F32)
        for t in range(TAPS):
            band = jnp.where(lane_id - row_id == t + 1, kx[v, t], band)
        band = band / jnp.full((B, Z), tap_sum(kx, v), F32)
        parts.append(jnp.where(inside, band, 0.0))
    full = jnp.concatenate(parts, axis=0)
    flipped = full.T[:COLS]
    keep_top = jnp.where(i == 0, 0.0, 1.0).astype(F32)
    keep_bottom = jnp.where(i == ny - 1, 0.0, 1.0).astype(F32)
    for n, keep in enumerate((None, keep_top, keep_bottom)):
        a = full if keep is None else full * keep
        b = flipped if keep is None else flipped * keep
        hi, lo = split(a[:, :COLS])
        tf[n, :, 0:COLS] = hi
        tf[n, :, COLS:2 * COLS] = hi
        tf[n, :, 2 * COLS:3 * COLS] = lo
        hi, lo = split(b)
        tb[n, :, 0:Z] = hi
        tb[n, :, Z:2 * Z] = hi
        tb[n, :, 2 * Z:3 * Z] = lo

    def depth_matrix(v, c):
        r = lax.broadcasted_iota(jnp.int32, (Z, Z), 0)
        l = lax.broadcasted_iota(jnp.int32, (Z, Z), 1)
        band = jnp.zeros((Z, Z), F32)
        for t in range(TAPS):
            band = jnp.where(r - l == t - RAD, kz[v, t], band)
        band = band / jnp.full((Z, Z), tap_sum(kz, v) * tap_sum(ky, v), F32)
        for ref, m in ((wf, band), (wb, band.T)):
            hi, lo = split(m)
            ref[v, 0:Z, :] = hi
            ref[v, Z:2 * Z, :] = hi
            ref[v, 2 * Z:3 * Z, :] = lo
        return c

    lax.fori_loop(0, VIEWS, depth_matrix, 0)

    def x_forward(start, count, n):
        data = jnp.concatenate([triple_rows(u[start + r]) for r in range(count)], axis=1)
        res = dot(tf[n], data)
        for r in range(count):
            xb[start + r] = res[:, r * Z:(r + 1) * Z]

    load_cur.wait()
    side_mate.wait_recv()
    side_away.wait_recv()

    def own_rows(g, c):
        x_forward(RAD + 4 * g, 4, 0)
        return c

    lax.fori_loop(0, B // 4, own_rows, 0)

    def y_forward_own(n, c):
        off = pl.ds(pl.multiple_of(n * 8, 8), 8)
        v = n // 4
        w = [ky[v, t] for t in range(TAPS)]
        for b in range(4):
            acc = [None] * 8
            for r in range(max(RAD, 8 * b), min(RAD + B - 1, 8 * b + 37) + 1):
                x = xb[r, off, :]
                for o in range(8):
                    t = r - (8 * b + o)
                    if 0 <= t < TAPS:
                        term = w[t] * x
                        acc[o] = term if acc[o] is None else acc[o] + term
            for o in range(8):
                yb[8 * b + o, off, :] = acc[o]
        return c

    lax.fori_loop(0, 16, y_forward_own, 0)

    down_mate.wait_recv()
    pass_top.start()
    up_mate.wait_recv()
    pass_bottom.start()
    down_away.wait_recv()
    up_away.wait_recv()
    diag_down.wait_recv()
    diag_up.wait_recv()
    pass_top.wait_recv()
    pass_bottom.wait_recv()

    def halo_rows(g, c):
        s = jnp.minimum(4 * g, RAD - 4)
        x_forward(s, 4, 1)
        x_forward(RAD + B + s, 4, 2)
        return c

    lax.fori_loop(0, 4, halo_rows, 0)

    def y_forward_halo(n, c):
        off = pl.ds(pl.multiple_of(n * 8, 8), 8)
        v = n // 4
        w = [ky[v, t] for t in range(TAPS)]
        for b in range(4):
            outs = [8 * b + o for o in range(8)]
            acc = {}
            for r in list(range(0, RAD)) + list(range(RAD + B, ROWS)):
                hits = [o for o in outs if 0 <= r - o < TAPS]
                if not hits:
                    continue
                x = xb[r, off, :]
                for o in hits:
                    term = w[r - o] * x
                    acc[o] = acc[o] + term if o in acc else term
            for o, a in acc.items():
                yb[o, off, :] += a
        return c

    lax.fori_loop(0, 16, y_forward_halo, 0)

    load_rec.wait()

    def depth(n, c):
        v = n // 4
        rows = pl.ds(pl.multiple_of(lax.rem(n, 4) * 8, 8), 8)
        lines = pl.ds(pl.multiple_of(v * B, B), B)
        blurred = dot(triple_lanes(yb[rows, lines, :].reshape(8 * B, Z)), wf[v])
        quotient = rv[v, rows].reshape(8 * B, Z) / blurred
        yb[rows, lines, :] = dot(triple_lanes(quotient), wb[v]).reshape(8, B, Z)
        return c

    lax.fori_loop(0, 16, depth, 0)

    def y_backward(rows):
        def step(n, c):
            off = pl.ds(pl.multiple_of(n * 8, 8), 8)
            v = n // 4
            w = [ky[v, t] for t in range(TAPS)]
            for group in rows:
                acc = {}
                for q in range(max(0, group[0] - TAPS + 1), min(B - 1, group[-1]) + 1):
                    x = yb[q, off, :]
                    for r in group:
                        if 0 <= r - q < TAPS:
                            term = w[r - q] * x
                            acc[r] = acc[r] + term if r in acc else term
                for r, a in acc.items():
                    xb[r, off, :] = a
            return c

        lax.fori_loop(0, 16, step, 0)

    def x_backward(start, count, n):
        data = jnp.concatenate([triple_rows(xb[start + r]) for r in range(count)], axis=1)
        res = dot(tb[n], data)
        for r in range(count):
            p[start + r] = res[:, r * Z:(r + 1) * Z]

    y_backward([range(0, 8), range(8, 15), range(47, 55), range(55, 62)])

    def halo_back(g, c):
        s = jnp.minimum(4 * g, RAD - 4)
        x_backward(s, 4, 1)
        x_backward(RAD + B + s, 4, 2)
        return c

    lax.fori_loop(0, 4, halo_back, 0)

    mate_top = remote(10, p.at[top, col(halo_mate), :], rpc.at[0], (i, mate))
    mate_bottom = remote(11, p.at[bottom, col(halo_mate), :], rpc.at[1], (i, mate))
    back_up_away = remote(12, p.at[top, col(H + own_away), :], ry.at[1, :, col(own_away), :], (up, j))
    back_down_away = remote(13, p.at[bottom, col(H + own_away), :], ry.at[0, :, col(own_away), :], (down, j))
    back_up_mate = remote(14, p.at[top, col(H + own_mate), :], ry.at[1, :, col(own_mate), :], (up, j))
    back_down_mate = remote(15, p.at[bottom, col(H + own_mate), :], ry.at[0, :, col(own_mate), :], (down, j))
    back_diag_up = remote(16, p.at[top, col(halo_away), :], rd.at[1], (up, away))
    back_diag_down = remote(17, p.at[bottom, col(halo_away), :], rd.at[0], (down, away))
    back_away = remote(18, p.at[mid, col(halo_away), :], rxo, (i, away))
    back_mate = remote(19, p.at[mid, col(halo_mate), :], rxp, (i, mate))
    mate_top.start()
    mate_bottom.start()
    back_up_away.start()
    back_down_away.start()
    mate_top.wait_recv()
    p[top, col(H + own_mate), :] += rpc[0]
    back_up_mate.start()
    mate_bottom.wait_recv()
    p[bottom, col(H + own_mate), :] += rpc[1]
    back_down_mate.start()
    back_diag_up.start()
    back_diag_down.start()

    y_backward([range(RAD + 8 * b, RAD + 8 * b + 8) for b in range(4)])

    def own_back(g, c):
        x_backward(RAD + 4 * g, 4, 0)
        return c

    lax.fori_loop(0, B // 4, own_back, 0)
    back_mate.start()
    back_away.start()

    back_mate.wait()
    p[mid, col(H + own_mate), :] += rxp[...]
    back_away.wait()
    p[mid, col(H + own_away), :] += rxo[...]
    back_diag_down.wait()
    p[pl.ds(RAD, RAD), col(H + own_away), :] += rd[0]
    back_diag_up.wait()
    p[pl.ds(B, RAD), col(H + own_away), :] += rd[1]
    for c in (back_down_away, back_down_mate, back_up_away, back_up_mate):
        c.wait()
    p[pl.ds(RAD, RAD), pl.ds(H, B), :] += ry[0]
    p[pl.ds(B, RAD), pl.ds(H, B), :] += ry[1]
    own = (pl.ds(RAD, B), pl.ds(H, B), slice(None))
    out[...] = u[own] * (p[own] * (1.0 / VIEWS))

    for c in (up_mate, down_mate, up_away, down_away, side_away, side_mate, diag_up, diag_down,
              pass_top, pass_bottom, mate_top, mate_bottom):
        c.wait_send()


def body(ny, nx, current, recorded, psf_depth, psf_rows, psf_cols):
    hbm = pl.BlockSpec(memory_space=pl.ANY)
    smem = pl.BlockSpec(memory_space=pltpu.SMEM)
    return pl.pallas_call(
        functools.partial(kernel, ny, nx),
        out_shape=jax.ShapeDtypeStruct((B, B, Z), F32),
        in_specs=[hbm, hbm, smem, smem, smem],
        out_specs=pl.BlockSpec(memory_space=pltpu.VMEM),
        scratch_shapes=[
            pltpu.VMEM((ROWS, COLS, Z), F32),
            pltpu.VMEM((ROWS, VIEWS * B, Z), F32),
            pltpu.VMEM((B, VIEWS * B, Z), F32),
            pltpu.VMEM((VIEWS, B, B, Z), F32),
            pltpu.VMEM((ROWS, COLS, Z), F32),
            pltpu.VMEM((2, RAD, B, Z), F32),
            pltpu.VMEM((B, H, Z), F32),
            pltpu.VMEM((B, H, Z), F32),
            pltpu.VMEM((2, RAD, H, Z), F32),
            pltpu.VMEM((2, RAD, H, Z), F32),
            pltpu.VMEM((3, VIEWS * B, 3 * COLS), BF16),
            pltpu.VMEM((3, COLS, 3 * Z), BF16),
            pltpu.VMEM((VIEWS, 3 * Z, Z), BF16),
            pltpu.VMEM((VIEWS, 3 * Z, Z), BF16),
            pltpu.SemaphoreType.DMA((2,)),
            pltpu.SemaphoreType.DMA((20,)),
            pltpu.SemaphoreType.DMA((20,)),
        ],
        compiler_params=pltpu.CompilerParams(
            collective_id=0, has_side_effects=True, vmem_limit_bytes=48 * 1024 * 1024),
        name="richardson_lucy",
    )(current, recorded, psf_depth, psf_rows, psf_cols)


def solution(mesh):
    placed = (P("gy", "gx", None), P(None, "gy", "gx", None), P(), P(), P())
    return jax.shard_map(
        functools.partial(body, mesh.shape["gy"], mesh.shape["gx"]),
        mesh=mesh, in_specs=placed, out_specs=P("gy", "gx", None), check_vma=False
    )
```

```python
import functools

import jax
import jax.numpy as jnp
from jax import lax
from jax.experimental import pallas as pl
from jax.experimental.pallas import tpu as pltpu
from jax.sharding import PartitionSpec as P

F32 = jnp.float32
BF16 = jnp.bfloat16
TAPS = 31
RAD = 15
VIEWS = 4
B = 32
H = 16
ROWS = B + 2 * RAD
COLS = B + 2 * H
Z = 128


def split(x):
    hi = x.astype(BF16)
    return hi, (x - hi.astype(F32)).astype(BF16)


def triple_rows(x):
    hi, lo = split(x)
    return jnp.concatenate([hi, lo, hi], axis=0)


def triple_lanes(x):
    hi, lo = split(x)
    return jnp.concatenate([hi, lo, hi], axis=1)


def dot(a, b):
    return jnp.dot(a, b, preferred_element_type=F32)


def tap_sum(ref, v):
    total = ref[v, 0]
    for t in range(1, TAPS):
        total = total + ref[v, t]
    return total


def kernel(ny, nx, cur, rec, kz, ky, kx, out, u, xb, yb, gb, rv, p, ry, rxp, rxo, rd, rpc,
           tf, tb, wf, wb, local_sem, send_sem, recv_sem):
    i = lax.axis_index("gy")
    j = lax.axis_index("gx")
    side = lax.rem(j, 2)
    up = lax.rem(i + ny - 1, ny)
    down = lax.rem(i + 1, ny)
    away = lax.rem(j + nx - 1 + 2 * side, nx)
    mate = j + 1 - 2 * side

    def col(x):
        return pl.ds(pl.multiple_of(x, H), H)

    own_away = H * side
    own_mate = H * (1 - side)
    halo_away = 48 * side
    halo_mate = 48 * (1 - side)

    load_rec = pltpu.make_async_copy(rec, rv, local_sem.at[0])
    load_cur = pltpu.make_async_copy(cur, u.at[pl.ds(RAD, B), pl.ds(H, B), :], local_sem.at[1])
    load_cur.start()
    load_rec.start()

    barrier = pltpu.get_barrier_semaphore()
    peers = [(up, j), (down, j), (i, away), (i, mate), (up, away), (down, away)]
    for peer in peers:
        pl.semaphore_signal(barrier, inc=1, device_id=peer, device_id_type=pl.DeviceIdType.MESH)
    row_id = lax.broadcasted_iota(jnp.int32, (B, Z), 0)
    lane_id = lax.broadcasted_iota(jnp.int32, (B, Z), 1)
    low = jnp.where(j == 0, H, 0)
    high = jnp.where(j == nx - 1, H + B, COLS)
    inside = (lane_id >= low) & (lane_id < high)
    parts = []
    for v in range(VIEWS):
        band = jnp.zeros((B, Z), F32)
        for t in range(TAPS):
            band = jnp.where(lane_id - row_id == t + 1, kx[v, t], band)
        band = band / jnp.full((B, Z), tap_sum(kx, v), F32)
        parts.append(jnp.where(inside, band, 0.0))
    full = jnp.concatenate(parts, axis=0)
    flipped = full.T[:COLS]
    keep_top = jnp.where(i == 0, 0.0, 1.0).astype(F32)
    keep_bottom = jnp.where(i == ny - 1, 0.0, 1.0).astype(F32)
    for n, keep in enumerate((None, keep_top, keep_bottom)):
        a = full if keep is None else full * keep
        b = flipped if keep is None else flipped * keep
        hi, lo = split(a[:, :COLS])
        tf[n, :, 0:COLS] = hi
        tf[n, :, COLS:2 * COLS] = hi
        tf[n, :, 2 * COLS:3 * COLS] = lo
        hi, lo = split(b)
        tb[n, :, 0:Z] = hi
        tb[n, :, Z:2 * Z] = hi
        tb[n, :, 2 * Z:3 * Z] = lo

    def depth_matrix(v, c):
        r = lax.broadcasted_iota(jnp.int32, (Z, Z), 0)
        l = lax.broadcasted_iota(jnp.int32, (Z, Z), 1)
        band = jnp.zeros((Z, Z), F32)
        for t in range(TAPS):
            band = jnp.where(r - l == t - RAD, kz[v, t], band)
        band = band / jnp.full((Z, Z), tap_sum(kz, v) * tap_sum(ky, v), F32)
        for ref, m in ((wf, band), (wb, band.T)):
            hi, lo = split(m)
            ref[v, 0:Z, :] = hi
            ref[v, Z:2 * Z, :] = hi
            ref[v, 2 * Z:3 * Z, :] = lo
        return c

    lax.fori_loop(0, VIEWS, depth_matrix, 0)

    pl.semaphore_wait(barrier, len(peers))

    def remote(k, src, dst, peer):
        return pltpu.make_async_remote_copy(
            src_ref=src, dst_ref=dst, send_sem=send_sem.at[k], recv_sem=recv_sem.at[k],
            device_id=peer, device_id_type=pl.DeviceIdType.MESH)

    top = pl.ds(0, RAD)
    bottom = pl.ds(RAD + B, RAD)
    mid = pl.ds(RAD, B)
    first = pl.ds(0, RAD)
    last = pl.ds(B - RAD, RAD)

    up_mate = remote(0, cur.at[first, col(own_mate), :], u.at[bottom, col(H + own_mate), :], (up, j))
    down_mate = remote(1, cur.at[last, col(own_mate), :], u.at[top, col(H + own_mate), :], (down, j))
    up_away = remote(2, cur.at[first, col(own_away), :], u.at[bottom, col(H + own_away), :], (up, j))
    down_away = remote(3, cur.at[last, col(own_away), :], u.at[top, col(H + own_away), :], (down, j))
    side_away = remote(4, cur.at[:, col(own_away), :], u.at[mid, col(48 - halo_away), :], (i, away))
    side_mate = remote(5, cur.at[:, col(own_mate), :], u.at[mid, col(48 - halo_mate), :], (i, mate))
    diag_up = remote(6, cur.at[first, col(own_away), :], u.at[bottom, col(48 - halo_away), :], (up, away))
    diag_down = remote(7, cur.at[last, col(own_away), :], u.at[top, col(48 - halo_away), :], (down, away))
    pass_top = remote(8, u.at[top, col(H + own_mate), :], u.at[top, col(48 - halo_mate), :], (i, mate))
    pass_bottom = remote(9, u.at[bottom, col(H + own_mate), :], u.at[bottom, col(48 - halo_mate), :], (i, mate))
    for c in (side_mate, side_away, up_mate, down_mate, up_away, down_away, diag_up, diag_down):
        c.start()

    def x_forward(start, count, n):
        data = jnp.concatenate([triple_rows(u[start + r]) for r in range(count)], axis=1)
        res = dot(tf[n], data)
        for r in range(count):
            xb[start + r] = res[:, r * Z:(r + 1) * Z]

    load_cur.wait()
    side_mate.wait_recv()
    side_away.wait_recv()

    def own_rows(g, c):
        x_forward(RAD + 4 * g, 4, 0)
        return c

    lax.fori_loop(0, B // 4, own_rows, 0)

    def y_forward_own(n, c):
        off = pl.ds(pl.multiple_of(n * 8, 8), 8)
        v = n // 4
        w = [ky[v, t] for t in range(TAPS)]
        for b in range(4):
            acc = [None] * 8
            for r in range(max(RAD, 8 * b), min(RAD + B - 1, 8 * b + 37) + 1):
                x = xb[r, off, :]
                for o in range(8):
                    t = r - (8 * b + o)
                    if 0 <= t < TAPS:
                        term = w[t] * x
                        acc[o] = term if acc[o] is None else acc[o] + term
            for o in range(8):
                yb[8 * b + o, off, :] = acc[o]
        return c

    lax.fori_loop(0, 16, y_forward_own, 0)

    down_mate.wait_recv()
    pass_top.start()
    up_mate.wait_recv()
    pass_bottom.start()
    down_away.wait_recv()
    up_away.wait_recv()
    diag_down.wait_recv()
    diag_up.wait_recv()
    pass_top.wait_recv()
    pass_bottom.wait_recv()

    def halo_rows(g, c):
        s = jnp.minimum(4 * g, RAD - 4)
        x_forward(s, 4, 1)
        x_forward(RAD + B + s, 4, 2)
        return c

    lax.fori_loop(0, 4, halo_rows, 0)

    def y_forward_halo(n, c):
        off = pl.ds(pl.multiple_of(n * 8, 8), 8)
        v = n // 4
        w = [ky[v, t] for t in range(TAPS)]
        for b in range(4):
            outs = [8 * b + o for o in range(8)]
            acc = {}
            for r in list(range(0, RAD)) + list(range(RAD + B, ROWS)):
                hits = [o for o in outs if 0 <= r - o < TAPS]
                if not hits:
                    continue
                x = xb[r, off, :]
                for o in hits:
                    term = w[r - o] * x
                    acc[o] = acc[o] + term if o in acc else term
            for o, a in acc.items():
                yb[o, off, :] += a
        return c

    lax.fori_loop(0, 16, y_forward_halo, 0)

    load_rec.wait()

    def depth(n, c):
        rows = pl.ds(pl.multiple_of(n * 8, 8), 8)
        lines = [pl.ds(v * B, B) for v in range(VIEWS)]
        data = [triple_lanes(yb[rows, lines[v], :].reshape(8 * B, Z)) for v in range(VIEWS)]
        blurred = [dot(data[v], wf[v]) for v in range(VIEWS)]
        data = [triple_lanes(rv[v, rows].reshape(8 * B, Z) / blurred[v]) for v in range(VIEWS)]
        res = [dot(data[v], wb[v]) for v in range(VIEWS)]
        for v in range(VIEWS):
            gb[rows, lines[v], :] = res[v].reshape(8, B, Z)
        return c

    lax.fori_loop(0, 4, depth, 0)

    def y_backward(rows):
        def step(n, c):
            off = pl.ds(pl.multiple_of(n * 8, 8), 8)
            v = n // 4
            w = [ky[v, t] for t in range(TAPS)]
            for group in rows:
                acc = {}
                for q in range(max(0, group[0] - TAPS + 1), min(B - 1, group[-1]) + 1):
                    x = gb[q, off, :]
                    for r in group:
                        if 0 <= r - q < TAPS:
                            term = w[r - q] * x
                            acc[r] = acc[r] + term if r in acc else term
                for r, a in acc.items():
                    xb[r, off, :] = a
            return c

        lax.fori_loop(0, 16, step, 0)

    def x_backward(start, count, n):
        data = jnp.concatenate([triple_rows(xb[start + r]) for r in range(count)], axis=1)
        res = dot(tb[n], data)
        for r in range(count):
            p[start + r] = res[:, r * Z:(r + 1) * Z]

    y_backward([range(0, 8), range(8, 15), range(47, 55), range(55, 62)])

    def halo_back(g, c):
        s = jnp.minimum(4 * g, RAD - 4)
        x_backward(s, 4, 1)
        x_backward(RAD + B + s, 4, 2)
        return c

    lax.fori_loop(0, 4, halo_back, 0)

    mate_top = remote(10, p.at[top, col(halo_mate), :], rpc.at[0], (i, mate))
    mate_bottom = remote(11, p.at[bottom, col(halo_mate), :], rpc.at[1], (i, mate))
    back_up_away = remote(12, p.at[top, col(H + own_away), :], ry.at[1, :, col(own_away), :], (up, j))
    back_down_away = remote(13, p.at[bottom, col(H + own_away), :], ry.at[0, :, col(own_away), :], (down, j))
    back_up_mate = remote(14, p.at[top, col(H + own_mate), :], ry.at[1, :, col(own_mate), :], (up, j))
    back_down_mate = remote(15, p.at[bottom, col(H + own_mate), :], ry.at[0, :, col(own_mate), :], (down, j))
    back_diag_up = remote(16, p.at[top, col(halo_away), :], rd.at[1], (up, away))
    back_diag_down = remote(17, p.at[bottom, col(halo_away), :], rd.at[0], (down, away))
    back_away = remote(18, p.at[mid, col(halo_away), :], rxo, (i, away))
    back_mate = remote(19, p.at[mid, col(halo_mate), :], rxp, (i, mate))
    mate_top.start()
    mate_bottom.start()
    back_up_away.start()
    back_down_away.start()
    mate_top.wait_recv()
    p[top, col(H + own_mate), :] += rpc[0]
    back_up_mate.start()
    mate_bottom.wait_recv()
    p[bottom, col(H + own_mate), :] += rpc[1]
    back_down_mate.start()
    back_diag_up.start()
    back_diag_down.start()

    y_backward([range(RAD + 8 * b, RAD + 8 * b + 8) for b in range(4)])

    def own_back(g, c):
        x_backward(RAD + 4 * g, 4, 0)
        return c

    lax.fori_loop(0, B // 4, own_back, 0)
    back_mate.start()
    back_away.start()

    back_mate.wait()
    p[mid, col(H + own_mate), :] += rxp[...]
    back_away.wait()
    p[mid, col(H + own_away), :] += rxo[...]
    back_diag_down.wait()
    p[pl.ds(RAD, RAD), col(H + own_away), :] += rd[0]
    back_diag_up.wait()
    p[pl.ds(B, RAD), col(H + own_away), :] += rd[1]
    for c in (back_down_away, back_down_mate, back_up_away, back_up_mate):
        c.wait()
    p[pl.ds(RAD, RAD), pl.ds(H, B), :] += ry[0]
    p[pl.ds(B, RAD), pl.ds(H, B), :] += ry[1]
    own = (pl.ds(RAD, B), pl.ds(H, B), slice(None))
    out[...] = u[own] * (p[own] * (1.0 / VIEWS))

    for c in (up_mate, down_mate, up_away, down_away, side_away, side_mate, diag_up, diag_down,
              pass_top, pass_bottom, mate_top, mate_bottom):
        c.wait_send()


def body(ny, nx, current, recorded, psf_depth, psf_rows, psf_cols):
    hbm = pl.BlockSpec(memory_space=pl.ANY)
    smem = pl.BlockSpec(memory_space=pltpu.SMEM)
    return pl.pallas_call(
        functools.partial(kernel, ny, nx),
        out_shape=jax.ShapeDtypeStruct((B, B, Z), F32),
        in_specs=[hbm, hbm, smem, smem, smem],
        out_specs=pl.BlockSpec(memory_space=pltpu.VMEM),
        scratch_shapes=[
            pltpu.VMEM((ROWS, COLS, Z), F32),
            pltpu.VMEM((ROWS, VIEWS * B, Z), F32),
            pltpu.VMEM((B, VIEWS * B, Z), F32),
            pltpu.VMEM((B, VIEWS * B, Z), F32),
            pltpu.VMEM((VIEWS, B, B, Z), F32),
            pltpu.VMEM((ROWS, COLS, Z), F32),
            pltpu.VMEM((2, RAD, B, Z), F32),
            pltpu.VMEM((B, H, Z), F32),
            pltpu.VMEM((B, H, Z), F32),
            pltpu.VMEM((2, RAD, H, Z), F32),
            pltpu.VMEM((2, RAD, H, Z), F32),
            pltpu.VMEM((3, VIEWS * B, 3 * COLS), BF16),
            pltpu.VMEM((3, COLS, 3 * Z), BF16),
            pltpu.VMEM((VIEWS, 3 * Z, Z), BF16),
            pltpu.VMEM((VIEWS, 3 * Z, Z), BF16),
            pltpu.SemaphoreType.DMA((2,)),
            pltpu.SemaphoreType.DMA((20,)),
            pltpu.SemaphoreType.DMA((20,)),
        ],
        compiler_params=pltpu.CompilerParams(
            collective_id=0, has_side_effects=True, vmem_limit_bytes=60 * 1024 * 1024),
        name="richardson_lucy",
    )(current, recorded, psf_depth, psf_rows, psf_cols)


def solution(mesh):
    placed = (P("gy", "gx", None), P(None, "gy", "gx", None), P(), P(), P())
    return jax.shard_map(
        functools.partial(body, mesh.shape["gy"], mesh.shape["gx"]),
        mesh=mesh, in_specs=placed, out_specs=P("gy", "gx", None), check_vma=False
    )
```

```python
import functools

import jax
import jax.numpy as jnp
from jax import lax
from jax.experimental import pallas as pl
from jax.experimental.pallas import tpu as pltpu
from jax.sharding import PartitionSpec as P

F32 = jnp.float32
BF16 = jnp.bfloat16
TAPS = 31
RAD = 15
VIEWS = 4
B = 32
H = 16
ROWS = B + 2 * RAD
COLS = B + 2 * H
Z = 128


def split(x):
    hi = x.astype(BF16)
    return hi, (x - hi.astype(F32)).astype(BF16)


def triple_rows(x):
    hi, lo = split(x)
    return jnp.concatenate([hi, lo, hi], axis=0)


def triple_lanes(x):
    hi, lo = split(x)
    return jnp.concatenate([hi, lo, hi], axis=1)


def dot(a, b):
    return jnp.dot(a, b, preferred_element_type=F32)


def tap_sum(ref, v):
    total = ref[v, 0]
    for t in range(1, TAPS):
        total = total + ref[v, t]
    return total


def kernel(ny, nx, cur, rec, kz, ky, kx, out, u, xb, yb, gb, rv, p, ry, rxp, rxo, rup, rdn, rq, rpc,
           tf, tb, wf, wb, local_sem, send_sem, recv_sem):
    i = lax.axis_index("gy")
    j = lax.axis_index("gx")
    side = lax.rem(j, 2)
    up = lax.rem(i + ny - 1, ny)
    down = lax.rem(i + 1, ny)
    away = lax.rem(j + nx - 1 + 2 * side, nx)
    mate = j + 1 - 2 * side

    def col(x):
        return pl.ds(pl.multiple_of(x, H), H)

    own_away = H * side
    own_mate = H * (1 - side)
    halo_away = 48 * side
    halo_mate = 48 * (1 - side)

    load_rec = pltpu.make_async_copy(rec, rv, local_sem.at[0])
    load_cur = pltpu.make_async_copy(cur, u.at[pl.ds(RAD, B), pl.ds(H, B), :], local_sem.at[1])
    load_cur.start()
    load_rec.start()

    barrier = pltpu.get_barrier_semaphore()
    peers = [(up, j), (down, j), (i, away), (i, mate), (up, away), (down, away)]
    for peer in peers:
        pl.semaphore_signal(barrier, inc=1, device_id=peer, device_id_type=pl.DeviceIdType.MESH)
    pl.semaphore_wait(barrier, len(peers))

    count = [0]

    def remote(src, dst, peer):
        k = count[0]
        count[0] += 1
        return pltpu.make_async_remote_copy(
            src_ref=src, dst_ref=dst, send_sem=send_sem.at[k], recv_sem=recv_sem.at[k],
            device_id=peer, device_id_type=pl.DeviceIdType.MESH)

    near_top, far_top = pl.ds(7, 8), pl.ds(0, 7)
    near_bottom, far_bottom = pl.ds(47, 8), pl.ds(55, 7)
    top, bottom, mid = pl.ds(0, RAD), pl.ds(RAD + B, RAD), pl.ds(RAD, B)
    to_top = ((pl.ds(24, 8), near_top), (pl.ds(17, 7), far_top))
    to_bottom = ((pl.ds(0, 8), near_bottom), (pl.ds(8, 7), far_bottom))
    mine = H + own_away
    theirs = 48 - mine
    side_mate = remote(cur.at[:, col(own_mate), :], u.at[mid, col(48 - halo_mate), :], (i, mate))

    def corner(rows, peer):
        return [remote(cur.at[a, col(own_away), :], u.at[b, col(48 - halo_away), :], (peer, away)) for a, b in rows]

    def edge(rows, peer):
        return [remote(cur.at[a, col(own_mate), :], u.at[b, col(H + own_mate), :], (peer, j)) for a, b in rows]

    corner_up, corner_down = corner(to_bottom, up), corner(to_top, down)
    edge_up, edge_down = edge(to_bottom, up), edge(to_top, down)
    side_away = [remote(cur.at[pl.ds(r, n), col(own_away), :], u.at[pl.ds(RAD + r, n), col(48 - halo_away), :], (i, away))
                 for r, n in ((24, 8), (17, 7), (0, 17))]
    relay_down = [remote(u.at[pl.ds(RAD + r, n), col(halo_away), :], u.at[b, col(theirs), :], (down, away))
                  for r, n, b in ((24, 8, near_top), (17, 7, far_top))]
    relay_away = [remote(u.at[b, col(halo_away), :], u.at[b, col(theirs), :], (i, away))
                  for b in (near_bottom, far_bottom)]
    pass_top = [remote(u.at[b, col(H + own_mate), :], u.at[b, col(48 - halo_mate), :], (i, mate))
                for b in (near_top, far_top)]
    pass_bottom = [remote(u.at[b, col(H + own_mate), :], u.at[b, col(48 - halo_mate), :], (i, mate))
                   for b in (near_bottom, far_bottom)]
    for c in (side_mate, corner_up[0], side_away[0], corner_up[1], side_away[1], side_away[2],
              edge_down[0], edge_up[0], corner_down[0], edge_down[1], edge_up[1], corner_down[1]):
        c.start()

    row_id = lax.broadcasted_iota(jnp.int32, (B, Z), 0)
    lane_id = lax.broadcasted_iota(jnp.int32, (B, Z), 1)
    low = jnp.where(j == 0, H, 0)
    high = jnp.where(j == nx - 1, H + B, COLS)
    inside = (lane_id >= low) & (lane_id < high)
    parts = []
    for v in range(VIEWS):
        band = jnp.zeros((B, Z), F32)
        for t in range(TAPS):
            band = jnp.where(lane_id - row_id == t + 1, kx[v, t], band)
        band = band / jnp.full((B, Z), tap_sum(kx, v), F32)
        parts.append(jnp.where(inside, band, 0.0))
    full = jnp.concatenate(parts, axis=0)
    flipped = full.T[:COLS]
    keep_top = jnp.where(i == 0, 0.0, 1.0).astype(F32)
    keep_bottom = jnp.where(i == ny - 1, 0.0, 1.0).astype(F32)
    for n, keep in enumerate((None, keep_top, keep_bottom)):
        a = full if keep is None else full * keep
        b = flipped if keep is None else flipped * keep
        hi, lo = split(a[:, :COLS])
        tf[n, :, 0:COLS] = hi
        tf[n, :, COLS:2 * COLS] = hi
        tf[n, :, 2 * COLS:3 * COLS] = lo
        hi, lo = split(b)
        tb[n, :, 0:Z] = hi
        tb[n, :, Z:2 * Z] = hi
        tb[n, :, 2 * Z:3 * Z] = lo

    def depth_matrix(v, c):
        r = lax.broadcasted_iota(jnp.int32, (Z, Z), 0)
        l = lax.broadcasted_iota(jnp.int32, (Z, Z), 1)
        band = jnp.zeros((Z, Z), F32)
        for t in range(TAPS):
            band = jnp.where(r - l == t - RAD, kz[v, t], band)
        band = band / jnp.full((Z, Z), tap_sum(kz, v) * tap_sum(ky, v), F32)
        for ref, m in ((wf, band), (wb, band.T)):
            hi, lo = split(m)
            ref[v, 0:Z, :] = hi
            ref[v, Z:2 * Z, :] = hi
            ref[v, 2 * Z:3 * Z, :] = lo
        return c

    lax.fori_loop(0, VIEWS, depth_matrix, 0)

    def x_forward(start, count, n):
        data = jnp.concatenate([triple_rows(u[start + r]) for r in range(count)], axis=1)
        res = dot(tf[n], data)
        for r in range(count):
            xb[start + r] = res[:, r * Z:(r + 1) * Z]

    for n in range(2):
        corner_up[n].wait_recv()
        relay_away[n].start()
        side_away[n].wait_recv()
        relay_down[n].start()
    load_cur.wait()
    side_mate.wait_recv()
    side_away[2].wait_recv()

    def own_rows(g, c):
        x_forward(RAD + 4 * g, 4, 0)
        return c

    lax.fori_loop(0, B // 4, own_rows, 0)

    edge_down[0].wait_recv()
    pass_top[0].start()
    edge_up[0].wait_recv()
    pass_bottom[0].start()

    def y_forward_own(n, c):
        off = pl.ds(pl.multiple_of(n * 8, 8), 8)
        v = n // 4
        w = [ky[v, t] for t in range(TAPS)]
        for b in range(4):
            acc = [None] * 8
            for r in range(max(RAD, 8 * b), min(RAD + B - 1, 8 * b + 37) + 1):
                x = xb[r, off, :]
                for o in range(8):
                    t = r - (8 * b + o)
                    if 0 <= t < TAPS:
                        term = w[t] * x
                        acc[o] = term if acc[o] is None else acc[o] + term
            for o in range(8):
                yb[8 * b + o, off, :] = acc[o]
        return c

    lax.fori_loop(0, 16, y_forward_own, 0)

    edge_down[1].wait_recv()
    pass_top[1].start()
    edge_up[1].wait_recv()
    pass_bottom[1].start()

    def arrived(n):
        for c in (corner_down[n], relay_away[n], relay_down[n], pass_top[n], pass_bottom[n]):
            c.wait_recv()

    def y_forward_halo(rows):
        def step(n, c):
            off = pl.ds(pl.multiple_of(n * 8, 8), 8)
            v = n // 4
            w = [ky[v, t] for t in range(TAPS)]
            for b in range(4):
                outs = [8 * b + o for o in range(8)]
                acc = {}
                for r in rows:
                    hits = [o for o in outs if 0 <= r - o < TAPS]
                    if not hits:
                        continue
                    x = xb[r, off, :]
                    for o in hits:
                        term = w[r - o] * x
                        acc[o] = acc[o] + term if o in acc else term
                for o, a in acc.items():
                    yb[o, off, :] += a
            return c

        lax.fori_loop(0, 16, step, 0)

    def depth(n, c):
        rows = pl.ds(pl.multiple_of(n * 8, 8), 8)
        lines = [pl.ds(v * B, B) for v in range(VIEWS)]
        data = [triple_lanes(yb[rows, lines[v], :].reshape(8 * B, Z)) for v in range(VIEWS)]
        blurred = [dot(data[v], wf[v]) for v in range(VIEWS)]
        data = [triple_lanes(rv[v, rows].reshape(8 * B, Z) / blurred[v]) for v in range(VIEWS)]
        res = [dot(data[v], wb[v]) for v in range(VIEWS)]
        for v in range(VIEWS):
            gb[rows, lines[v], :] = res[v].reshape(8, B, Z)
        return c

    def near_rows(g, c):
        x_forward(7 + 4 * g, 4, 1)
        x_forward(47 + 4 * g, 4, 2)
        return c

    def far_rows(g, c):
        x_forward(3 * g, 4, 1)
        x_forward(55 + 3 * g, 4, 2)
        return c

    arrived(0)
    lax.fori_loop(0, 2, near_rows, 0)
    y_forward_halo(list(range(7, 15)) + list(range(47, 55)))
    load_rec.wait()
    lax.fori_loop(1, 3, depth, 0)
    arrived(1)
    lax.fori_loop(0, 2, far_rows, 0)
    y_forward_halo(list(range(0, 7)) + list(range(55, 62)))
    lax.fori_loop(0, 2, lambda n, c: depth(3 * n, c), 0)

    def y_backward(rows):
        def step(n, c):
            off = pl.ds(pl.multiple_of(n * 8, 8), 8)
            v = n // 4
            w = [ky[v, t] for t in range(TAPS)]
            for group in rows:
                acc = {}
                for q in range(max(0, group[0] - TAPS + 1), min(B - 1, group[-1]) + 1):
                    x = gb[q, off, :]
                    for r in group:
                        if 0 <= r - q < TAPS:
                            term = w[r - q] * x
                            acc[r] = acc[r] + term if r in acc else term
                for r, a in acc.items():
                    xb[r, off, :] = a
            return c

        lax.fori_loop(0, 16, step, 0)

    def x_backward(start, count, n):
        data = jnp.concatenate([triple_rows(xb[start + r]) for r in range(count)], axis=1)
        res = dot(tb[n], data)
        for r in range(count):
            p[start + r] = res[:, r * Z:(r + 1) * Z]

    wide = pl.ds(pl.multiple_of(32 * side, 32), B)
    mate_bottom = remote(p.at[bottom, col(halo_mate), :], rpc.at[1], (i, mate))
    mate_top = remote(p.at[top, col(halo_mate), :], rpc.at[0], (i, mate))
    sum_away = remote(p.at[bottom, col(mine), :], rq, (i, away))
    sum_up = remote(p.at[top, wide, :], rup, (up, away))
    sum_down = remote(p.at[bottom, col(halo_away), :], rdn, (down, away))
    back_up = remote(p.at[top, col(H + own_mate), :], ry.at[1], (up, j))
    back_down = remote(p.at[bottom, col(H + own_mate), :], ry.at[0], (down, j))
    back_mate = remote(p.at[mid, col(halo_mate), :], rxp, (i, mate))
    upper, lower = pl.ds(RAD, B - RAD), pl.ds(B, RAD)
    back_away = [remote(p.at[a, col(halo_away), :], rxo.at[b], (i, away))
                 for a, b in ((upper, pl.ds(0, B - RAD)), (lower, pl.ds(B - RAD, RAD)))]

    def halo_back(start, n):
        def step(g, c):
            x_backward(start + jnp.minimum(4 * g, RAD - 4), 4, n)
            return c

        lax.fori_loop(0, 4, step, 0)

    y_backward([range(47, 55), range(55, 62)])
    halo_back(RAD + B, 2)
    sum_away.start()
    mate_bottom.start()
    y_backward([range(0, 8), range(8, 15)])
    halo_back(0, 1)
    sum_up.start()
    mate_top.start()
    mate_bottom.wait_recv()
    p[bottom, col(H + own_mate), :] += rpc[1]
    back_down.start()
    mate_top.wait_recv()
    p[top, col(H + own_mate), :] += rpc[0]
    back_up.start()

    y_backward([range(RAD + 8 * b, RAD + 8 * b + 8) for b in range(4)])
    sum_away.wait_recv()
    p[bottom, col(halo_away), :] += rq[...]
    sum_down.start()

    def own_back(g, c):
        x_backward(RAD + 4 * g, 4, 0)
        return c

    lax.fori_loop(0, B // 4, own_back, 0)
    back_away[0].start()
    back_mate.start()
    sum_up.wait_recv()
    p[lower, wide, :] += rup[...]
    back_away[1].start()

    back_mate.wait_recv()
    p[mid, col(H + own_mate), :] += rxp[...]
    back_down.wait_recv()
    p[pl.ds(RAD, RAD), col(H + own_mate), :] += ry[0]
    back_up.wait_recv()
    p[lower, col(H + own_mate), :] += ry[1]
    sum_down.wait_recv()
    p[pl.ds(RAD, RAD), col(mine), :] += rdn[...]
    back_away[0].wait_recv()
    back_away[1].wait_recv()
    p[mid, col(mine), :] += rxo[...]
    own = (mid, pl.ds(H, B), slice(None))
    out[...] = u[own] * (p[own] * (1.0 / VIEWS))

    for c in (side_mate, *corner_up, *corner_down, *edge_up, *edge_down, *side_away, *relay_down, *relay_away,
              *pass_top, *pass_bottom, mate_bottom, mate_top, sum_away, sum_up, sum_down, back_up, back_down,
              back_mate, *back_away):
        c.wait_send()


def body(ny, nx, current, recorded, psf_depth, psf_rows, psf_cols):
    hbm = pl.BlockSpec(memory_space=pl.ANY)
    smem = pl.BlockSpec(memory_space=pltpu.SMEM)
    return pl.pallas_call(
        functools.partial(kernel, ny, nx),
        out_shape=jax.ShapeDtypeStruct((B, B, Z), F32),
        in_specs=[hbm, hbm, smem, smem, smem],
        out_specs=pl.BlockSpec(memory_space=pltpu.VMEM),
        scratch_shapes=[
            pltpu.VMEM((ROWS, COLS, Z), F32),
            pltpu.VMEM((ROWS, VIEWS * B, Z), F32),
            pltpu.VMEM((B, VIEWS * B, Z), F32),
            pltpu.VMEM((B, VIEWS * B, Z), F32),
            pltpu.VMEM((VIEWS, B, B, Z), F32),
            pltpu.VMEM((ROWS, COLS, Z), F32),
            pltpu.VMEM((2, RAD, H, Z), F32),
            pltpu.VMEM((B, H, Z), F32),
            pltpu.VMEM((B, H, Z), F32),
            pltpu.VMEM((RAD, B, Z), F32),
            pltpu.VMEM((RAD, H, Z), F32),
            pltpu.VMEM((RAD, H, Z), F32),
            pltpu.VMEM((2, RAD, H, Z), F32),
            pltpu.VMEM((3, VIEWS * B, 3 * COLS), BF16),
            pltpu.VMEM((3, COLS, 3 * Z), BF16),
            pltpu.VMEM((VIEWS, 3 * Z, Z), BF16),
            pltpu.VMEM((VIEWS, 3 * Z, Z), BF16),
            pltpu.SemaphoreType.DMA((2,)),
            pltpu.SemaphoreType.DMA((32,)),
            pltpu.SemaphoreType.DMA((32,)),
        ],
        compiler_params=pltpu.CompilerParams(
            collective_id=0, has_side_effects=True, vmem_limit_bytes=60 * 1024 * 1024),
        name="richardson_lucy",
    )(current, recorded, psf_depth, psf_rows, psf_cols)


def solution(mesh):
    placed = (P("gy", "gx", None), P(None, "gy", "gx", None), P(), P(), P())
    return jax.shard_map(
        functools.partial(body, mesh.shape["gy"], mesh.shape["gx"]),
        mesh=mesh, in_specs=placed, out_specs=P("gy", "gx", None), check_vma=False
    )
```

```python
import functools

import jax
import jax.numpy as jnp
from jax import lax
from jax.experimental import pallas as pl
from jax.experimental.pallas import tpu as pltpu
from jax.sharding import PartitionSpec as P

F32 = jnp.float32
BF16 = jnp.bfloat16
TAPS = 31
RAD = 15
VIEWS = 4
B = 32
H = 16
HL = 64
ROWS = B + 2 * RAD
COLS = B + 2 * H
Z = 128


def split(x):
    hi = x.astype(BF16)
    return hi, (x - hi.astype(F32)).astype(BF16)


def triple_rows(x):
    hi, lo = split(x)
    return jnp.concatenate([hi, lo, hi], axis=0)


def triple_lanes(x):
    hi, lo = split(x)
    return jnp.concatenate([hi, lo, hi], axis=1)


def dot(a, b):
    return jnp.dot(a, b, preferred_element_type=F32)


def tap_sum(ref, v):
    total = ref[v, 0]
    for t in range(1, TAPS):
        total = total + ref[v, t]
    return total


def kernel(ny, nx, cur, rec, kz, ky, kx, out, u, xb, yb, gb, rv, p, ry, rxp, rxo, rup, rdn, rq, rpc,
           tf, tfm, tb, wf, wb, local_sem, send_sem, recv_sem):
    i = lax.axis_index("gy")
    j = lax.axis_index("gx")
    side = lax.rem(j, 2)
    up = lax.rem(i + ny - 1, ny)
    down = lax.rem(i + 1, ny)
    away = lax.rem(j + nx - 1 + 2 * side, nx)
    mate = j + 1 - 2 * side

    def col(x):
        return pl.ds(pl.multiple_of(x, H), H)

    own_away = H * side
    own_mate = H * (1 - side)
    halo_away = 48 * side
    halo_mate = 48 * (1 - side)

    load_rec = pltpu.make_async_copy(rec, rv, local_sem.at[0])
    load_cur = pltpu.make_async_copy(cur, u.at[pl.ds(RAD, B), pl.ds(H, B), :], local_sem.at[1])
    load_cur.start()
    load_rec.start()

    barrier = pltpu.get_barrier_semaphore()
    peers = [(up, j), (down, j), (i, away), (i, mate), (up, away), (down, away)]
    for peer in peers:
        pl.semaphore_signal(barrier, inc=1, device_id=peer, device_id_type=pl.DeviceIdType.MESH)
    pl.semaphore_wait(barrier, len(peers))

    count = [0]

    def remote(src, dst, peer):
        k = count[0]
        count[0] += 1
        return pltpu.make_async_remote_copy(
            src_ref=src, dst_ref=dst, send_sem=send_sem.at[k], recv_sem=recv_sem.at[k],
            device_id=peer, device_id_type=pl.DeviceIdType.MESH)

    near_top, far_top = pl.ds(7, 8), pl.ds(0, 7)
    near_bottom, far_bottom = pl.ds(47, 8), pl.ds(55, 7)
    top, bottom, mid = pl.ds(0, RAD), pl.ds(RAD + B, RAD), pl.ds(RAD, B)
    to_top = ((pl.ds(24, 8), near_top), (pl.ds(17, 7), far_top))
    to_bottom = ((pl.ds(0, 8), near_bottom), (pl.ds(8, 7), far_bottom))
    mine = H + own_away
    theirs = 48 - mine
    side_mate = remote(cur.at[:, col(own_mate), :], u.at[mid, col(48 - halo_mate), :], (i, mate))

    def corner(rows, peer):
        return [remote(cur.at[a, col(own_away), :], u.at[b, col(48 - halo_away), :], (peer, away)) for a, b in rows]

    def edge(rows, peer):
        return [remote(cur.at[a, col(own_mate), :], u.at[b, col(H + own_mate), :], (peer, j)) for a, b in rows]

    corner_up, corner_down = corner(to_bottom, up), corner(to_top, down)
    edge_up, edge_down = edge(to_bottom, up), edge(to_top, down)
    side_away = [remote(cur.at[pl.ds(r, n), col(own_away), :], u.at[pl.ds(RAD + r, n), col(48 - halo_away), :], (i, away))
                 for r, n in ((24, 8), (17, 7), (0, 17))]
    relay_down = [remote(u.at[pl.ds(RAD + r, n), col(halo_away), :], u.at[b, col(theirs), :], (down, away))
                  for r, n, b in ((24, 8, near_top), (17, 7, far_top))]
    relay_away = [remote(u.at[b, col(halo_away), :], u.at[b, col(theirs), :], (i, away))
                  for b in (near_bottom, far_bottom)]
    pass_top = [remote(u.at[b, col(H + own_mate), :], u.at[b, col(48 - halo_mate), :], (i, mate))
                for b in (near_top, far_top)]
    pass_bottom = [remote(u.at[b, col(H + own_mate), :], u.at[b, col(48 - halo_mate), :], (i, mate))
                   for b in (near_bottom, far_bottom)]
    side_mate.start()
    corner_up[0].start()
    side_away[0].start()
    corner_up[1].start()
    side_away[1].start()
    side_away[2].start()
    edge_down[0].start()
    edge_up[0].start()
    corner_down[0].start()

    row_id = lax.broadcasted_iota(jnp.int32, (H, Z), 0)
    lane_id = lax.broadcasted_iota(jnp.int32, (H, Z), 1)
    low = jnp.where(j == 0, H, 0)
    high = jnp.where(j == nx - 1, H + B, COLS)
    def column_bands(half, base):
        parts = []
        for v in range(VIEWS):
            band = jnp.zeros((H, Z), F32)
            for t in range(TAPS):
                band = jnp.where(lane_id - row_id == half - base + t + 1, kx[v, t], band)
            band = band / jnp.full((H, Z), tap_sum(kx, v), F32)
            parts.append(jnp.where((lane_id >= low - base) & (lane_id < high - base), band, 0.0))
        return jnp.concatenate(parts, axis=0)

    full = jnp.concatenate([column_bands(own_mate, 0), column_bands(own_away, 0)], axis=0)
    hi, lo = split(column_bands(own_mate, own_mate)[:, :COLS])
    tfm[:, 0:COLS] = hi
    tfm[:, COLS:2 * COLS] = hi
    tfm[:, 2 * COLS:3 * COLS] = lo
    flipped = full.T[:COLS]
    keep_top = jnp.where(i == 0, 0.0, 1.0).astype(F32)
    keep_bottom = jnp.where(i == ny - 1, 0.0, 1.0).astype(F32)
    for n, keep in enumerate((None, keep_top, keep_bottom)):
        a = full if keep is None else full * keep
        b = flipped if keep is None else flipped * keep
        hi, lo = split(a[:, :COLS])
        tf[n, :, 0:COLS] = hi
        tf[n, :, COLS:2 * COLS] = hi
        tf[n, :, 2 * COLS:3 * COLS] = lo
        hi, lo = split(b)
        tb[n, :, 0:Z] = hi
        tb[n, :, Z:2 * Z] = hi
        tb[n, :, 2 * Z:3 * Z] = lo

    def depth_matrix(v, c):
        r = lax.broadcasted_iota(jnp.int32, (Z, Z), 0)
        l = lax.broadcasted_iota(jnp.int32, (Z, Z), 1)
        band = jnp.zeros((Z, Z), F32)
        for t in range(TAPS):
            band = jnp.where(r - l == t - RAD, kz[v, t], band)
        band = band / jnp.full((Z, Z), tap_sum(kz, v) * tap_sum(ky, v), F32)
        for ref, m in ((wf, band), (wb, band.T)):
            hi, lo = split(m)
            ref[v, 0:Z, :] = hi
            ref[v, Z:2 * Z, :] = hi
            ref[v, 2 * Z:3 * Z, :] = lo
        return c

    lax.fori_loop(0, VIEWS, depth_matrix, 0)

    def x_forward(start, count, n, lines=(0, 2 * HL)):
        data = jnp.concatenate([triple_rows(u[start + r]) for r in range(count)], axis=1)
        res = dot(tf[n, lines[0]:lines[1]], data)
        for r in range(count):
            xb[start + r, lines[0]:lines[1]] = res[:, r * Z:(r + 1) * Z]

    def mate_rows():
        def step(g, c):
            reach = pl.ds(pl.multiple_of(own_mate, H), 3 * H)
            none = jnp.zeros((H, Z), F32)
            data = jnp.concatenate(
                [triple_rows(jnp.concatenate([u[RAD + 4 * g + r, reach, :], none], axis=0)) for r in range(4)], axis=1)
            res = dot(tfm[...], data)
            for r in range(4):
                xb[RAD + 4 * g + r, 0:HL] = res[:, r * Z:(r + 1) * Z]
            return c

        lax.fori_loop(0, B // 4, step, 0)

    def own_rows(lines):
        def step(g, c):
            x_forward(RAD + 4 * g, 4, 0, lines)
            return c

        lax.fori_loop(0, B // 4, step, 0)

    def y_forward_own(n, c):
        off = pl.ds(pl.multiple_of(n * 8, 8), 8)
        v = lax.rem(n // 2, VIEWS)
        w = [ky[v, t] for t in range(TAPS)]
        for b in range(4):
            acc = [None] * 8
            for r in range(max(RAD, 8 * b), min(RAD + B - 1, 8 * b + 37) + 1):
                x = xb[r, off, :]
                for o in range(8):
                    t = r - (8 * b + o)
                    if 0 <= t < TAPS:
                        term = w[t] * x
                        acc[o] = term if acc[o] is None else acc[o] + term
            for o in range(8):
                yb[8 * b + o, off, :] = acc[o]
        return c

    load_cur.wait()
    side_mate.wait_recv()
    mate_rows()
    lax.fori_loop(0, 8, y_forward_own, 0)
    corner_up[0].wait_recv()
    relay_away[0].start()
    side_away[0].wait_recv()
    relay_down[0].start()
    corner_up[1].wait_recv()
    side_away[1].wait_recv()
    side_away[2].wait_recv()
    edge_down[1].start()
    edge_up[1].start()
    corner_down[1].start()
    relay_away[1].start()
    relay_down[1].start()
    own_rows((HL, 2 * HL))
    lax.fori_loop(8, 16, y_forward_own, 0)
    edge_down[0].wait_recv()
    pass_top[0].start()
    edge_up[0].wait_recv()
    pass_bottom[0].start()
    edge_down[1].wait_recv()
    pass_top[1].start()
    edge_up[1].wait_recv()
    pass_bottom[1].start()

    def arrived(n):
        for c in (corner_down[n], relay_away[n], relay_down[n], pass_top[n], pass_bottom[n]):
            c.wait_recv()

    def y_forward_halo(rows):
        def step(n, c):
            off = pl.ds(pl.multiple_of(n * 8, 8), 8)
            v = lax.rem(n // 2, VIEWS)
            w = [ky[v, t] for t in range(TAPS)]
            for b in range(4):
                outs = [8 * b + o for o in range(8)]
                acc = {}
                for r in rows:
                    hits = [o for o in outs if 0 <= r - o < TAPS]
                    if not hits:
                        continue
                    x = xb[r, off, :]
                    for o in hits:
                        term = w[r - o] * x
                        acc[o] = acc[o] + term if o in acc else term
                for o, a in acc.items():
                    yb[o, off, :] += a
            return c

        lax.fori_loop(0, 16, step, 0)

    def depth(n, c):
        rows = pl.ds(pl.multiple_of(n * 8, 8), 8)
        lines = [[pl.ds(h * HL + v * H, H) for h in range(2)] for v in range(VIEWS)]
        halves = (col(own_mate), col(own_away))

        def flat(x, y):
            return jnp.concatenate([x.reshape(8 * H, Z), y.reshape(8 * H, Z)], axis=0)

        data = [triple_lanes(flat(*(yb[rows, q, :] for q in lines[v]))) for v in range(VIEWS)]
        blurred = [dot(data[v], wf[v]) for v in range(VIEWS)]
        images = [flat(*(rv[v, rows, q, :] for q in halves)) for v in range(VIEWS)]
        data = [triple_lanes(images[v] / blurred[v]) for v in range(VIEWS)]
        res = [dot(data[v], wb[v]) for v in range(VIEWS)]
        for v in range(VIEWS):
            for h in range(2):
                gb[rows, lines[v][h], :] = res[v][h * 8 * H:(h + 1) * 8 * H].reshape(8, H, Z)
        return c

    def near_rows(g, c):
        x_forward(7 + 4 * g, 4, 1)
        x_forward(47 + 4 * g, 4, 2)
        return c

    def far_rows(g, c):
        x_forward(3 * g, 4, 1)
        x_forward(55 + 3 * g, 4, 2)
        return c

    arrived(0)
    lax.fori_loop(0, 2, near_rows, 0)
    y_forward_halo(list(range(7, 15)) + list(range(47, 55)))
    load_rec.wait()
    lax.fori_loop(1, 3, depth, 0)
    arrived(1)
    lax.fori_loop(0, 2, far_rows, 0)
    y_forward_halo(list(range(0, 7)) + list(range(55, 62)))
    lax.fori_loop(0, 2, lambda n, c: depth(3 * n, c), 0)

    def y_backward(rows):
        def step(n, c):
            off = pl.ds(pl.multiple_of(n * 8, 8), 8)
            v = lax.rem(n // 2, VIEWS)
            w = [ky[v, t] for t in range(TAPS)]
            for group in rows:
                acc = {}
                for q in range(max(0, group[0] - TAPS + 1), min(B - 1, group[-1]) + 1):
                    x = gb[q, off, :]
                    for r in group:
                        if 0 <= r - q < TAPS:
                            term = w[r - q] * x
                            acc[r] = acc[r] + term if r in acc else term
                for r, a in acc.items():
                    xb[r, off, :] = a
            return c

        lax.fori_loop(0, 16, step, 0)

    def x_backward(start, count, n):
        data = jnp.concatenate([triple_rows(xb[start + r]) for r in range(count)], axis=1)
        res = dot(tb[n], data)
        for r in range(count):
            p[start + r] = res[:, r * Z:(r + 1) * Z]

    mate_bottom = remote(p.at[bottom, col(halo_mate), :], rpc.at[1], (i, mate))
    mate_top = remote(p.at[top, col(halo_mate), :], rpc.at[0], (i, mate))
    sum_away = remote(p.at[bottom, col(mine), :], rq, (i, away))
    sum_up = remote(p.at[top, col(mine), :], rup.at[0], (up, away))
    sum_corner = remote(p.at[top, col(halo_away), :], rup.at[1], (up, away))
    sum_down = remote(p.at[bottom, col(halo_away), :], rdn, (down, away))
    back_up = remote(p.at[top, col(H + own_mate), :], ry.at[1], (up, j))
    back_down = remote(p.at[bottom, col(H + own_mate), :], ry.at[0], (down, j))
    back_mate = remote(p.at[mid, col(halo_mate), :], rxp, (i, mate))
    upper, lower = pl.ds(RAD, B - RAD), pl.ds(B, RAD)
    back_away = [remote(p.at[a, col(halo_away), :], rxo.at[b], (i, away))
                 for a, b in ((upper, pl.ds(0, B - RAD)), (lower, pl.ds(B - RAD, RAD)))]

    def halo_back(start, n):
        def step(g, c):
            x_backward(start + jnp.minimum(4 * g, RAD - 4), 4, n)
            return c

        lax.fori_loop(0, 4, step, 0)

    y_backward([range(47, 55), range(55, 62)])
    halo_back(RAD + B, 2)
    sum_away.start()
    mate_bottom.start()
    y_backward([range(0, 8), range(8, 15)])
    halo_back(0, 1)
    sum_up.start()
    mate_top.start()
    mate_bottom.wait_recv()
    p[bottom, col(H + own_mate), :] += rpc[1]
    back_down.start()
    mate_top.wait_recv()
    p[top, col(H + own_mate), :] += rpc[0]
    back_up.start()
    sum_corner.start()

    y_backward([range(RAD + 8 * b, RAD + 8 * b + 8) for b in range(4)])
    sum_away.wait_recv()
    p[bottom, col(halo_away), :] += rq[...]
    sum_down.start()

    def own_back(g, c):
        x_backward(RAD + 4 * g, 4, 0)
        return c

    lax.fori_loop(0, B // 4, own_back, 0)
    back_away[0].start()
    back_mate.start()
    sum_up.wait_recv()
    p[lower, col(halo_away), :] += rup[0]
    back_away[1].start()

    back_mate.wait_recv()
    p[mid, col(H + own_mate), :] += rxp[...]
    back_down.wait_recv()
    p[pl.ds(RAD, RAD), col(H + own_mate), :] += ry[0]
    back_up.wait_recv()
    p[lower, col(H + own_mate), :] += ry[1]
    sum_corner.wait_recv()
    p[lower, col(mine), :] += rup[1]
    sum_down.wait_recv()
    p[pl.ds(RAD, RAD), col(mine), :] += rdn[...]
    back_away[0].wait_recv()
    back_away[1].wait_recv()
    p[mid, col(mine), :] += rxo[...]
    own = (mid, pl.ds(H, B), slice(None))
    out[...] = u[own] * (p[own] * (1.0 / VIEWS))

    for c in (side_mate, *corner_up, *corner_down, *edge_up, *edge_down, *side_away, *relay_down, *relay_away,
              *pass_top, *pass_bottom, mate_bottom, mate_top, sum_away, sum_up, sum_corner, sum_down, back_up, back_down,
              back_mate, *back_away):
        c.wait_send()


def body(ny, nx, current, recorded, psf_depth, psf_rows, psf_cols):
    hbm = pl.BlockSpec(memory_space=pl.ANY)
    smem = pl.BlockSpec(memory_space=pltpu.SMEM)
    return pl.pallas_call(
        functools.partial(kernel, ny, nx),
        out_shape=jax.ShapeDtypeStruct((B, B, Z), F32),
        in_specs=[hbm, hbm, smem, smem, smem],
        out_specs=pl.BlockSpec(memory_space=pltpu.VMEM),
        scratch_shapes=[
            pltpu.VMEM((ROWS, COLS, Z), F32),
            pltpu.VMEM((ROWS, VIEWS * B, Z), F32),
            pltpu.VMEM((B, VIEWS * B, Z), F32),
            pltpu.VMEM((B, VIEWS * B, Z), F32),
            pltpu.VMEM((VIEWS, B, B, Z), F32),
            pltpu.VMEM((ROWS, COLS, Z), F32),
            pltpu.VMEM((2, RAD, H, Z), F32),
            pltpu.VMEM((B, H, Z), F32),
            pltpu.VMEM((B, H, Z), F32),
            pltpu.VMEM((2, RAD, H, Z), F32),
            pltpu.VMEM((RAD, H, Z), F32),
            pltpu.VMEM((RAD, H, Z), F32),
            pltpu.VMEM((2, RAD, H, Z), F32),
            pltpu.VMEM((3, VIEWS * B, 3 * COLS), BF16),
            pltpu.VMEM((HL, 3 * COLS), BF16),
            pltpu.VMEM((3, COLS, 3 * Z), BF16),
            pltpu.VMEM((VIEWS, 3 * Z, Z), BF16),
            pltpu.VMEM((VIEWS, 3 * Z, Z), BF16),
            pltpu.SemaphoreType.DMA((2,)),
            pltpu.SemaphoreType.DMA((32,)),
            pltpu.SemaphoreType.DMA((32,)),
        ],
        compiler_params=pltpu.CompilerParams(
            collective_id=0, has_side_effects=True, vmem_limit_bytes=60 * 1024 * 1024),
        name="richardson_lucy",
    )(current, recorded, psf_depth, psf_rows, psf_cols)


def solution(mesh):
    placed = (P("gy", "gx", None), P(None, "gy", "gx", None), P(), P(), P())
    return jax.shard_map(
        functools.partial(body, mesh.shape["gy"], mesh.shape["gx"]),
        mesh=mesh, in_specs=placed, out_specs=P("gy", "gx", None), check_vma=False
    )
```

```python
import functools

import jax
import jax.numpy as jnp
from jax import lax
from jax.experimental import pallas as pl
from jax.experimental.pallas import tpu as pltpu
from jax.sharding import PartitionSpec as P

F32 = jnp.float32
BF16 = jnp.bfloat16
TAPS = 31
RAD = 15
VIEWS = 4
B = 32
H = 16
HL = 64
ROWS = B + 2 * RAD
COLS = B + 2 * H
Z = 128


def split(x):
    hi = x.astype(BF16)
    return hi, (x - hi.astype(F32)).astype(BF16)


def triple_rows(x):
    hi, lo = split(x)
    return jnp.concatenate([hi, lo, hi], axis=0)


def triple_lanes(x):
    hi, lo = split(x)
    return jnp.concatenate([hi, lo, hi], axis=1)


def dot(a, b):
    return jnp.dot(a, b, preferred_element_type=F32)


def tap_sum(ref, v):
    total = ref[v, 0]
    for t in range(1, TAPS):
        total = total + ref[v, t]
    return total


def kernel(ny, nx, cur, rec, kz, ky, kx, out, u, xb, yb, gb, rv, p, ry, rxp, rxo, rup, rdn, rq, rpc,
           tf, tfm, tb, wf, wb, local_sem, send_sem, recv_sem):
    i = lax.axis_index("gy")
    j = lax.axis_index("gx")
    side = lax.rem(j, 2)
    up = lax.rem(i + ny - 1, ny)
    down = lax.rem(i + 1, ny)
    away = lax.rem(j + nx - 1 + 2 * side, nx)
    mate = j + 1 - 2 * side

    def col(x):
        return pl.ds(pl.multiple_of(x, H), H)

    own_away = H * side
    own_mate = H * (1 - side)
    halo_away = 48 * side
    halo_mate = 48 * (1 - side)

    load_rec = pltpu.make_async_copy(rec, rv, local_sem.at[0])
    load_cur = pltpu.make_async_copy(cur, u.at[pl.ds(RAD, B), pl.ds(H, B), :], local_sem.at[1])
    load_cur.start()
    load_rec.start()

    barrier = pltpu.get_barrier_semaphore()
    peers = [(up, j), (down, j), (i, away), (i, mate), (up, away), (down, away)]
    for peer in peers:
        pl.semaphore_signal(barrier, inc=1, device_id=peer, device_id_type=pl.DeviceIdType.MESH)
    pl.semaphore_wait(barrier, len(peers))

    count = [0]

    def remote(src, dst, peer):
        k = count[0]
        count[0] += 1
        return pltpu.make_async_remote_copy(
            src_ref=src, dst_ref=dst, send_sem=send_sem.at[k], recv_sem=recv_sem.at[k],
            device_id=peer, device_id_type=pl.DeviceIdType.MESH)

    near_top, far_top = pl.ds(7, 8), pl.ds(0, 7)
    near_bottom, far_bottom = pl.ds(47, 8), pl.ds(55, 7)
    top, bottom, mid = pl.ds(0, RAD), pl.ds(RAD + B, RAD), pl.ds(RAD, B)
    to_top = ((pl.ds(24, 8), near_top), (pl.ds(17, 7), far_top))
    to_bottom = ((pl.ds(0, 8), near_bottom), (pl.ds(8, 7), far_bottom))
    mine = H + own_away
    theirs = 48 - mine
    side_mate = remote(cur.at[:, col(own_mate), :], u.at[mid, col(48 - halo_mate), :], (i, mate))

    def corner(rows, peer):
        return [remote(cur.at[a, col(own_away), :], u.at[b, col(48 - halo_away), :], (peer, away)) for a, b in rows]

    def edge(rows, peer):
        return [remote(cur.at[a, col(own_mate), :], u.at[b, col(H + own_mate), :], (peer, j)) for a, b in rows]

    corner_up, corner_down = corner(to_bottom, up), corner(to_top, down)
    edge_up, edge_down = edge(to_bottom, up), edge(to_top, down)
    side_away = [remote(cur.at[pl.ds(r, n), col(own_away), :], u.at[pl.ds(RAD + r, n), col(48 - halo_away), :], (i, away))
                 for r, n in ((24, 8), (17, 7), (0, 17))]
    relay_down = [remote(u.at[pl.ds(RAD + r, n), col(halo_away), :], u.at[b, col(theirs), :], (down, away))
                  for r, n, b in ((24, 8, near_top), (17, 7, far_top))]
    relay_away = [remote(u.at[b, col(halo_away), :], u.at[b, col(theirs), :], (i, away))
                  for b in (near_bottom, far_bottom)]
    pass_top = [remote(u.at[b, col(H + own_mate), :], u.at[b, col(48 - halo_mate), :], (i, mate))
                for b in (near_top, far_top)]
    pass_bottom = [remote(u.at[b, col(H + own_mate), :], u.at[b, col(48 - halo_mate), :], (i, mate))
                   for b in (near_bottom, far_bottom)]
    side_mate.start()
    corner_up[0].start()
    side_away[0].start()
    corner_up[1].start()
    side_away[1].start()
    side_away[2].start()
    edge_down[0].start()
    edge_up[0].start()
    corner_down[0].start()

    row_id = lax.broadcasted_iota(jnp.int32, (H, Z), 0)
    lane_id = lax.broadcasted_iota(jnp.int32, (H, Z), 1)
    low = jnp.where(j == 0, H, 0)
    high = jnp.where(j == nx - 1, H + B, COLS)
    def column_bands(half, base):
        parts = []
        for v in range(VIEWS):
            band = jnp.zeros((H, Z), F32)
            for t in range(TAPS):
                band = jnp.where(lane_id - row_id == half - base + t + 1, kx[v, t], band)
            band = band / jnp.full((H, Z), tap_sum(kx, v), F32)
            parts.append(jnp.where((lane_id >= low - base) & (lane_id < high - base), band, 0.0))
        return jnp.concatenate(parts, axis=0)

    full = jnp.concatenate([column_bands(own_mate, 0), column_bands(own_away, 0)], axis=0)
    hi, lo = split(column_bands(own_mate, own_mate)[:, :COLS])
    tfm[:, 0:COLS] = hi
    tfm[:, COLS:2 * COLS] = hi
    tfm[:, 2 * COLS:3 * COLS] = lo
    flipped = full.T[:COLS]
    keep_top = jnp.where(i == 0, 0.0, 1.0).astype(F32)
    keep_bottom = jnp.where(i == ny - 1, 0.0, 1.0).astype(F32)
    for n, keep in enumerate((None, keep_top, keep_bottom)):
        a = full if keep is None else full * keep
        b = flipped if keep is None else flipped * keep
        hi, lo = split(a[:, :COLS])
        tf[n, :, 0:COLS] = hi
        tf[n, :, COLS:2 * COLS] = hi
        tf[n, :, 2 * COLS:3 * COLS] = lo
        hi, lo = split(b)
        tb[n, :, 0:Z] = hi
        tb[n, :, Z:2 * Z] = hi
        tb[n, :, 2 * Z:3 * Z] = lo

    def depth_matrix(v, c):
        r = lax.broadcasted_iota(jnp.int32, (Z, Z), 0)
        l = lax.broadcasted_iota(jnp.int32, (Z, Z), 1)
        band = jnp.zeros((Z, Z), F32)
        for t in range(TAPS):
            band = jnp.where(r - l == t - RAD, kz[v, t], band)
        band = band / jnp.full((Z, Z), tap_sum(kz, v) * tap_sum(ky, v), F32)
        for ref, m in ((wf, band), (wb, band.T)):
            hi, lo = split(m)
            ref[v, 0:Z, :] = hi
            ref[v, Z:2 * Z, :] = hi
            ref[v, 2 * Z:3 * Z, :] = lo
        return c

    lax.fori_loop(0, VIEWS, depth_matrix, 0)

    def x_forward(start, count, n, lines=(0, 2 * HL)):
        data = jnp.concatenate([triple_rows(u[start + r]) for r in range(count)], axis=1)
        res = dot(tf[n, lines[0]:lines[1]], data)
        for r in range(count):
            xb[start + r, lines[0]:lines[1]] = res[:, r * Z:(r + 1) * Z]

    def mate_rows():
        def step(g, c):
            reach = pl.ds(pl.multiple_of(own_mate, H), 3 * H)
            none = jnp.zeros((H, Z), F32)
            data = jnp.concatenate(
                [triple_rows(jnp.concatenate([u[RAD + 4 * g + r, reach, :], none], axis=0)) for r in range(4)], axis=1)
            res = dot(tfm[...], data)
            for r in range(4):
                xb[RAD + 4 * g + r, 0:HL] = res[:, r * Z:(r + 1) * Z]
            return c

        lax.fori_loop(0, B // 4, step, 0)

    def own_rows(lines):
        def step(g, c):
            x_forward(RAD + 4 * g, 4, 0, lines)
            return c

        lax.fori_loop(0, B // 4, step, 0)

    def y_forward_own(n, c):
        off = pl.ds(pl.multiple_of(n * 8, 8), 8)
        v = lax.rem(n // 2, VIEWS)
        w = [ky[v, t] for t in range(TAPS)]
        for b in range(4):
            acc = [None] * 8
            for r in range(max(RAD, 8 * b), min(RAD + B - 1, 8 * b + 37) + 1):
                x = xb[r, off, :]
                for o in range(8):
                    t = r - (8 * b + o)
                    if 0 <= t < TAPS:
                        term = w[t] * x
                        acc[o] = term if acc[o] is None else acc[o] + term
            for o in range(8):
                yb[8 * b + o, off, :] = acc[o]
        return c

    load_cur.wait()
    side_mate.wait_recv()
    mate_rows()
    lax.fori_loop(0, 8, y_forward_own, 0)
    corner_up[0].wait_recv()
    relay_away[0].start()
    side_away[0].wait_recv()
    relay_down[0].start()
    corner_up[1].wait_recv()
    side_away[1].wait_recv()
    side_away[2].wait_recv()
    edge_down[1].start()
    edge_up[1].start()
    corner_down[1].start()
    relay_away[1].start()
    relay_down[1].start()
    own_rows((HL, 2 * HL))
    lax.fori_loop(8, 16, y_forward_own, 0)
    edge_down[0].wait_recv()
    pass_top[0].start()
    edge_up[0].wait_recv()
    pass_bottom[0].start()
    edge_down[1].wait_recv()
    pass_top[1].start()
    edge_up[1].wait_recv()
    pass_bottom[1].start()

    def y_forward_halo(rows):
        def step(n, c):
            off = pl.ds(pl.multiple_of(n * 8, 8), 8)
            v = lax.rem(n // 2, VIEWS)
            w = [ky[v, t] for t in range(TAPS)]
            for b in range(4):
                outs = [8 * b + o for o in range(8)]
                acc = {}
                for r in rows:
                    hits = [o for o in outs if 0 <= r - o < TAPS]
                    if not hits:
                        continue
                    x = xb[r, off, :]
                    for o in hits:
                        term = w[r - o] * x
                        acc[o] = acc[o] + term if o in acc else term
                for o, a in acc.items():
                    yb[o, off, :] += a
            return c

        lax.fori_loop(0, 16, step, 0, unroll=2)

    def depth(n, c):
        rows = pl.ds(pl.multiple_of(n * 8, 8), 8)
        lines = [[pl.ds(h * HL + v * H, H) for h in range(2)] for v in range(VIEWS)]
        halves = (col(own_mate), col(own_away))

        def flat(x, y):
            return jnp.concatenate([x.reshape(8 * H, Z), y.reshape(8 * H, Z)], axis=0)

        data = [triple_lanes(flat(*(yb[rows, q, :] for q in lines[v]))) for v in range(VIEWS)]
        blurred = [dot(data[v], wf[v]) for v in range(VIEWS)]
        images = [flat(*(rv[v, rows, q, :] for q in halves)) for v in range(VIEWS)]
        data = [triple_lanes(images[v] / blurred[v]) for v in range(VIEWS)]
        res = [dot(data[v], wb[v]) for v in range(VIEWS)]
        for v in range(VIEWS):
            for h in range(2):
                gb[rows, lines[v][h], :] = res[v][h * 8 * H:(h + 1) * 8 * H].reshape(8, H, Z)
        return c

    def near_rows(g, c):
        x_forward(7 + 4 * g, 4, 1)
        x_forward(47 + 4 * g, 4, 2)
        return c

    def far_rows(start, n):
        x_forward(start, 4, n)
        x_forward(start + 3, 4, n)

    for c in (corner_down[0], relay_away[0], relay_down[0], pass_top[0], pass_bottom[0]):
        c.wait_recv()
    lax.fori_loop(0, 2, near_rows, 0, unroll=2)
    y_forward_halo(list(range(7, 15)) + list(range(47, 55)))
    load_rec.wait()
    lax.fori_loop(1, 3, depth, 0)
    def y_backward(rows):
        def step(n, c):
            off = pl.ds(pl.multiple_of(n * 8, 8), 8)
            v = lax.rem(n // 2, VIEWS)
            w = [ky[v, t] for t in range(TAPS)]
            for group in rows:
                acc = {}
                for q in range(max(0, group[0] - TAPS + 1), min(B - 1, group[-1]) + 1):
                    x = gb[q, off, :]
                    for r in group:
                        if 0 <= r - q < TAPS:
                            term = w[r - q] * x
                            acc[r] = acc[r] + term if r in acc else term
                for r, a in acc.items():
                    xb[r, off, :] = a
            return c

        lax.fori_loop(0, 16, step, 0, unroll=2)

    def x_backward(start, count, n):
        data = jnp.concatenate([triple_rows(xb[start + r]) for r in range(count)], axis=1)
        res = dot(tb[n], data)
        for r in range(count):
            p[start + r] = res[:, r * Z:(r + 1) * Z]

    mate_bottom = remote(p.at[bottom, col(halo_mate), :], rpc.at[1], (i, mate))
    mate_top = remote(p.at[top, col(halo_mate), :], rpc.at[0], (i, mate))
    sum_away = remote(p.at[bottom, col(mine), :], rq, (i, away))
    sum_up = remote(p.at[top, col(mine), :], rup.at[0], (up, away))
    sum_corner = remote(p.at[top, col(halo_away), :], rup.at[1], (up, away))
    sum_down = remote(p.at[bottom, col(halo_away), :], rdn, (down, away))
    back_up = remote(p.at[top, col(H + own_mate), :], ry.at[1], (up, j))
    back_down = remote(p.at[bottom, col(H + own_mate), :], ry.at[0], (down, j))
    back_mate = remote(p.at[mid, col(halo_mate), :], rxp, (i, mate))
    upper, lower = pl.ds(RAD, B - RAD), pl.ds(B, RAD)
    back_away = [remote(p.at[a, col(halo_away), :], rxo.at[b], (i, away))
                 for a, b in ((upper, pl.ds(0, B - RAD)), (lower, pl.ds(B - RAD, RAD)))]

    def halo_back(start, n):
        def step(g, c):
            x_backward(start + jnp.minimum(4 * g, RAD - 4), 4, n)
            return c

        lax.fori_loop(0, 4, step, 0, unroll=4)

    relay_away[1].wait_recv()
    pass_bottom[1].wait_recv()
    far_rows(55, 2)
    y_forward_halo(list(range(55, 62)))
    depth(3, 0)
    y_backward([range(47, 55), range(55, 62)])
    halo_back(RAD + B, 2)
    sum_away.start()
    mate_bottom.start()
    for c in (corner_down[1], relay_down[1], pass_top[1]):
        c.wait_recv()
    far_rows(0, 1)
    y_forward_halo(list(range(0, 7)))
    depth(0, 0)
    mate_bottom.wait_recv()
    p[bottom, col(H + own_mate), :] += rpc[1]
    back_down.start()
    y_backward([range(0, 8), range(8, 15)])
    halo_back(0, 1)
    sum_up.start()
    mate_top.start()
    sum_away.wait_recv()
    p[bottom, col(halo_away), :] += rq[...]
    sum_down.start()
    mate_top.wait_recv()
    p[top, col(H + own_mate), :] += rpc[0]
    back_up.start()
    sum_corner.start()

    y_backward([range(RAD + 8 * b, RAD + 8 * b + 8) for b in range(4)])

    def own_back(g, c):
        x_backward(RAD + 4 * g, 4, 0)
        return c

    lax.fori_loop(0, B // 4, own_back, 0)
    back_away[0].start()
    back_mate.start()
    sum_up.wait_recv()
    p[lower, col(halo_away), :] += rup[0]
    back_away[1].start()

    back_mate.wait_recv()
    p[mid, col(H + own_mate), :] += rxp[...]
    back_down.wait_recv()
    p[pl.ds(RAD, RAD), col(H + own_mate), :] += ry[0]
    back_up.wait_recv()
    p[lower, col(H + own_mate), :] += ry[1]
    sum_corner.wait_recv()
    p[lower, col(mine), :] += rup[1]
    sum_down.wait_recv()
    p[pl.ds(RAD, RAD), col(mine), :] += rdn[...]
    back_away[0].wait_recv()
    back_away[1].wait_recv()
    p[mid, col(mine), :] += rxo[...]
    own = (mid, pl.ds(H, B), slice(None))
    out[...] = u[own] * (p[own] * (1.0 / VIEWS))

    for c in (side_mate, *corner_up, *corner_down, *edge_up, *edge_down, *side_away, *relay_down, *relay_away,
              *pass_top, *pass_bottom, mate_bottom, mate_top, sum_away, sum_up, sum_corner, sum_down, back_up, back_down,
              back_mate, *back_away):
        c.wait_send()


def body(ny, nx, current, recorded, psf_depth, psf_rows, psf_cols):
    hbm = pl.BlockSpec(memory_space=pl.ANY)
    smem = pl.BlockSpec(memory_space=pltpu.SMEM)
    return pl.pallas_call(
        functools.partial(kernel, ny, nx),
        out_shape=jax.ShapeDtypeStruct((B, B, Z), F32),
        in_specs=[hbm, hbm, smem, smem, smem],
        out_specs=pl.BlockSpec(memory_space=pltpu.VMEM),
        scratch_shapes=[
            pltpu.VMEM((ROWS, COLS, Z), F32),
            pltpu.VMEM((ROWS, VIEWS * B, Z), F32),
            pltpu.VMEM((B, VIEWS * B, Z), F32),
            pltpu.VMEM((B, VIEWS * B, Z), F32),
            pltpu.VMEM((VIEWS, B, B, Z), F32),
            pltpu.VMEM((ROWS, COLS, Z), F32),
            pltpu.VMEM((2, RAD, H, Z), F32),
            pltpu.VMEM((B, H, Z), F32),
            pltpu.VMEM((B, H, Z), F32),
            pltpu.VMEM((2, RAD, H, Z), F32),
            pltpu.VMEM((RAD, H, Z), F32),
            pltpu.VMEM((RAD, H, Z), F32),
            pltpu.VMEM((2, RAD, H, Z), F32),
            pltpu.VMEM((3, VIEWS * B, 3 * COLS), BF16),
            pltpu.VMEM((HL, 3 * COLS), BF16),
            pltpu.VMEM((3, COLS, 3 * Z), BF16),
            pltpu.VMEM((VIEWS, 3 * Z, Z), BF16),
            pltpu.VMEM((VIEWS, 3 * Z, Z), BF16),
            pltpu.SemaphoreType.DMA((2,)),
            pltpu.SemaphoreType.DMA((32,)),
            pltpu.SemaphoreType.DMA((32,)),
        ],
        compiler_params=pltpu.CompilerParams(
            collective_id=0, has_side_effects=True, vmem_limit_bytes=60 * 1024 * 1024),
        name="richardson_lucy",
    )(current, recorded, psf_depth, psf_rows, psf_cols)


def solution(mesh):
    placed = (P("gy", "gx", None), P(None, "gy", "gx", None), P(), P(), P())
    return jax.shard_map(
        functools.partial(body, mesh.shape["gy"], mesh.shape["gx"]),
        mesh=mesh, in_specs=placed, out_specs=P("gy", "gx", None), check_vma=False
    )
```

```python
import functools

import jax
import jax.numpy as jnp
from jax import lax
from jax.experimental import pallas as pl
from jax.experimental.pallas import tpu as pltpu
from jax.sharding import PartitionSpec as P

F32 = jnp.float32
BF16 = jnp.bfloat16
TAPS = 31
RAD = 15
VIEWS = 4
B = 32
H = 16
HL = 64
ROWS = B + 2 * RAD
COLS = B + 2 * H
Z = 128


def split(x):
    hi = x.astype(BF16)
    return hi, (x - hi.astype(F32)).astype(BF16)


def triple_rows(x):
    hi, lo = split(x)
    return jnp.concatenate([hi, lo, hi], axis=0)


def triple_lanes(x):
    hi, lo = split(x)
    return jnp.concatenate([hi, lo, hi], axis=1)


def dot(a, b):
    return jnp.dot(a, b, preferred_element_type=F32)


def tap_sum(ref, v):
    total = ref[v, 0]
    for t in range(1, TAPS):
        total = total + ref[v, t]
    return total


def kernel(ny, nx, cur, rec, kz, ky, kx, out, u, xb, yb, gb, rv, p, ry, rxp, rxo, rup, rdn, rq, rpc,
           tf, tfm, tb, wf, wb, local_sem, send_sem, recv_sem):
    i = lax.axis_index("gy")
    j = lax.axis_index("gx")
    side = lax.rem(j, 2)
    up = lax.rem(i + ny - 1, ny)
    down = lax.rem(i + 1, ny)
    away = lax.rem(j + nx - 1 + 2 * side, nx)
    mate = j + 1 - 2 * side

    def col(x):
        return pl.ds(pl.multiple_of(x, H), H)

    own_away = H * side
    own_mate = H * (1 - side)
    halo_away = 48 * side
    halo_mate = 48 * (1 - side)

    load_rec = pltpu.make_async_copy(rec, rv, local_sem.at[0])
    load_cur = pltpu.make_async_copy(cur, u.at[pl.ds(RAD, B), pl.ds(H, B), :], local_sem.at[1])
    load_cur.start()
    load_rec.start()

    barrier = pltpu.get_barrier_semaphore()
    peers = [(up, j), (down, j), (i, away), (i, mate), (up, away), (down, away)]
    for peer in peers:
        pl.semaphore_signal(barrier, inc=1, device_id=peer, device_id_type=pl.DeviceIdType.MESH)
    pl.semaphore_wait(barrier, len(peers))

    count = [0]

    def remote(src, dst, peer):
        k = count[0]
        count[0] += 1
        return pltpu.make_async_remote_copy(
            src_ref=src, dst_ref=dst, send_sem=send_sem.at[k], recv_sem=recv_sem.at[k],
            device_id=peer, device_id_type=pl.DeviceIdType.MESH)

    near_top, far_top = pl.ds(7, 8), pl.ds(0, 7)
    near_bottom, far_bottom = pl.ds(47, 8), pl.ds(55, 7)
    top, bottom, mid = pl.ds(0, RAD), pl.ds(RAD + B, RAD), pl.ds(RAD, B)
    to_top = ((pl.ds(24, 8), near_top), (pl.ds(17, 7), far_top))
    to_bottom = ((pl.ds(0, 8), near_bottom), (pl.ds(8, 7), far_bottom))
    mine = H + own_away
    theirs = 48 - mine
    side_mate = remote(cur.at[:, col(own_mate), :], u.at[mid, col(48 - halo_mate), :], (i, mate))

    def corner(rows, peer):
        return [remote(cur.at[a, col(own_away), :], u.at[b, col(48 - halo_away), :], (peer, away)) for a, b in rows]

    def edge(rows, peer):
        return [remote(cur.at[a, col(own_mate), :], u.at[b, col(H + own_mate), :], (peer, j)) for a, b in rows]

    corner_up, corner_down = corner(to_bottom, up), corner(to_top, down)
    edge_up, edge_down = edge(to_bottom, up), edge(to_top, down)
    side_away = [remote(cur.at[pl.ds(r, n), col(own_away), :], u.at[pl.ds(RAD + r, n), col(48 - halo_away), :], (i, away))
                 for r, n in ((24, 8), (17, 7), (0, 17))]
    relay_down = [remote(u.at[pl.ds(RAD + r, n), col(halo_away), :], u.at[b, col(theirs), :], (down, away))
                  for r, n, b in ((24, 8, near_top), (17, 7, far_top))]
    relay_away = [remote(u.at[b, col(halo_away), :], u.at[b, col(theirs), :], (i, away))
                  for b in (near_bottom, far_bottom)]
    pass_top = [remote(u.at[b, col(H + own_mate), :], u.at[b, col(48 - halo_mate), :], (i, mate))
                for b in (near_top, far_top)]
    pass_bottom = [remote(u.at[b, col(H + own_mate), :], u.at[b, col(48 - halo_mate), :], (i, mate))
                   for b in (near_bottom, far_bottom)]
    side_mate.start()
    corner_up[0].start()
    corner_up[1].start()
    side_away[0].start()
    side_away[1].start()
    side_away[2].start()
    edge_up[0].start()
    edge_up[1].start()

    row_id = lax.broadcasted_iota(jnp.int32, (H, Z), 0)
    lane_id = lax.broadcasted_iota(jnp.int32, (H, Z), 1)
    low = jnp.where(j == 0, H, 0)
    high = jnp.where(j == nx - 1, H + B, COLS)
    def column_bands(half, base):
        parts = []
        for v in range(VIEWS):
            band = jnp.zeros((H, Z), F32)
            for t in range(TAPS):
                band = jnp.where(lane_id - row_id == half - base + t + 1, kx[v, t], band)
            band = band / jnp.full((H, Z), tap_sum(kx, v), F32)
            parts.append(jnp.where((lane_id >= low - base) & (lane_id < high - base), band, 0.0))
        return jnp.concatenate(parts, axis=0)

    full = jnp.concatenate([column_bands(own_mate, 0), column_bands(own_away, 0)], axis=0)
    hi, lo = split(column_bands(own_mate, own_mate)[:, :COLS])
    tfm[:, 0:COLS] = hi
    tfm[:, COLS:2 * COLS] = hi
    tfm[:, 2 * COLS:3 * COLS] = lo
    flipped = full.T[:COLS]
    keep_top = jnp.where(i == 0, 0.0, 1.0).astype(F32)
    keep_bottom = jnp.where(i == ny - 1, 0.0, 1.0).astype(F32)
    for n, keep in enumerate((None, keep_top, keep_bottom)):
        a = full if keep is None else full * keep
        b = flipped if keep is None else flipped * keep
        hi, lo = split(a[:, :COLS])
        tf[n, :, 0:COLS] = hi
        tf[n, :, COLS:2 * COLS] = hi
        tf[n, :, 2 * COLS:3 * COLS] = lo
        hi, lo = split(b)
        tb[n, :, 0:Z] = hi
        tb[n, :, Z:2 * Z] = hi
        tb[n, :, 2 * Z:3 * Z] = lo

    def depth_matrix(v, c):
        r = lax.broadcasted_iota(jnp.int32, (Z, Z), 0)
        l = lax.broadcasted_iota(jnp.int32, (Z, Z), 1)
        band = jnp.zeros((Z, Z), F32)
        for t in range(TAPS):
            band = jnp.where(r - l == t - RAD, kz[v, t], band)
        band = band / jnp.full((Z, Z), tap_sum(kz, v) * tap_sum(ky, v), F32)
        for ref, m in ((wf, band), (wb, band.T)):
            hi, lo = split(m)
            ref[v, 0:Z, :] = hi
            ref[v, Z:2 * Z, :] = hi
            ref[v, 2 * Z:3 * Z, :] = lo
        return c

    lax.fori_loop(0, VIEWS, depth_matrix, 0)

    def x_forward(start, count, n, lines=(0, 2 * HL)):
        data = jnp.concatenate([triple_rows(u[start + r]) for r in range(count)], axis=1)
        res = dot(tf[n, lines[0]:lines[1]], data)
        for r in range(count):
            xb[start + r, lines[0]:lines[1]] = res[:, r * Z:(r + 1) * Z]

    def mate_rows():
        def step(g, c):
            reach = pl.ds(pl.multiple_of(own_mate, H), 3 * H)
            none = jnp.zeros((H, Z), F32)
            data = jnp.concatenate(
                [triple_rows(jnp.concatenate([u[RAD + 4 * g + r, reach, :], none], axis=0)) for r in range(4)], axis=1)
            res = dot(tfm[...], data)
            for r in range(4):
                xb[RAD + 4 * g + r, 0:HL] = res[:, r * Z:(r + 1) * Z]
            return c

        lax.fori_loop(0, B // 4, step, 0)

    def own_rows(lines):
        def step(g, c):
            x_forward(RAD + 4 * g, 4, 0, lines)
            return c

        lax.fori_loop(0, B // 4, step, 0)

    def y_forward_own(n, c):
        off = pl.ds(pl.multiple_of(n * 8, 8), 8)
        v = lax.rem(n // 2, VIEWS)
        w = [ky[v, t] for t in range(TAPS)]
        for b in range(4):
            acc = [None] * 8
            for r in range(max(RAD, 8 * b), min(RAD + B - 1, 8 * b + 37) + 1):
                x = xb[r, off, :]
                for o in range(8):
                    t = r - (8 * b + o)
                    if 0 <= t < TAPS:
                        term = w[t] * x
                        acc[o] = term if acc[o] is None else acc[o] + term
            for o in range(8):
                yb[8 * b + o, off, :] = acc[o]
        return c

    load_cur.wait()
    side_mate.wait_recv()
    mate_rows()
    lax.fori_loop(0, 8, y_forward_own, 0)
    corner_up[0].wait_recv()
    corner_up[1].wait_recv()
    relay_away[0].start()
    relay_away[1].start()
    corner_down[0].start()
    corner_down[1].start()
    side_away[0].wait_recv()
    relay_down[0].start()
    side_away[1].wait_recv()
    relay_down[1].start()
    side_away[2].wait_recv()
    edge_down[0].start()
    edge_down[1].start()
    own_rows((HL, 2 * HL))
    lax.fori_loop(8, 16, y_forward_own, 0)
    edge_up[0].wait_recv()
    pass_bottom[0].start()
    edge_up[1].wait_recv()
    pass_bottom[1].start()

    def y_forward_halo(rows):
        def step(n, c):
            off = pl.ds(pl.multiple_of(n * 8, 8), 8)
            v = lax.rem(n // 2, VIEWS)
            w = [ky[v, t] for t in range(TAPS)]
            for b in range(4):
                outs = [8 * b + o for o in range(8)]
                acc = {}
                for r in rows:
                    hits = [o for o in outs if 0 <= r - o < TAPS]
                    if not hits:
                        continue
                    x = xb[r, off, :]
                    for o in hits:
                        term = w[r - o] * x
                        acc[o] = acc[o] + term if o in acc else term
                for o, a in acc.items():
                    yb[o, off, :] += a
            return c

        lax.fori_loop(0, 16, step, 0, unroll=2)

    def depth(n, c):
        rows = pl.ds(pl.multiple_of(n * 8, 8), 8)
        lines = [[pl.ds(h * HL + v * H, H) for h in range(2)] for v in range(VIEWS)]
        halves = (col(own_mate), col(own_away))

        def flat(x, y):
            return jnp.concatenate([x.reshape(8 * H, Z), y.reshape(8 * H, Z)], axis=0)

        data = [triple_lanes(flat(*(yb[rows, q, :] for q in lines[v]))) for v in range(VIEWS)]
        blurred = [dot(data[v], wf[v]) for v in range(VIEWS)]
        images = [flat(*(rv[v, rows, q, :] for q in halves)) for v in range(VIEWS)]
        data = [triple_lanes(images[v] / blurred[v]) for v in range(VIEWS)]
        res = [dot(data[v], wb[v]) for v in range(VIEWS)]
        for v in range(VIEWS):
            for h in range(2):
                gb[rows, lines[v][h], :] = res[v][h * 8 * H:(h + 1) * 8 * H].reshape(8, H, Z)
        return c

    def edge_rows(start, n):
        for g in (0, 4, 8, RAD - 4):
            x_forward(start + g, 4, n)

    def y_backward(rows):
        def step(n, c):
            off = pl.ds(pl.multiple_of(n * 8, 8), 8)
            v = lax.rem(n // 2, VIEWS)
            w = [ky[v, t] for t in range(TAPS)]
            for group in rows:
                acc = {}
                for q in range(max(0, group[0] - TAPS + 1), min(B - 1, group[-1]) + 1):
                    x = gb[q, off, :]
                    for r in group:
                        if 0 <= r - q < TAPS:
                            term = w[r - q] * x
                            acc[r] = acc[r] + term if r in acc else term
                for r, a in acc.items():
                    xb[r, off, :] = a
            return c

        lax.fori_loop(0, 16, step, 0, unroll=2)

    def x_backward(start, count, n):
        data = jnp.concatenate([triple_rows(xb[start + r]) for r in range(count)], axis=1)
        res = dot(tb[n], data)
        for r in range(count):
            p[start + r] = res[:, r * Z:(r + 1) * Z]

    mate_bottom = remote(p.at[bottom, col(halo_mate), :], rpc.at[1], (i, mate))
    mate_top = remote(p.at[top, col(halo_mate), :], rpc.at[0], (i, mate))
    sum_away = remote(p.at[bottom, col(mine), :], rq, (i, away))
    sum_up = remote(p.at[top, col(mine), :], rup.at[0], (up, away))
    sum_corner = remote(p.at[top, col(halo_away), :], rup.at[1], (up, away))
    sum_down = remote(p.at[bottom, col(halo_away), :], rdn, (down, away))
    back_up = remote(p.at[top, col(H + own_mate), :], ry.at[1], (up, j))
    back_down = remote(p.at[bottom, col(H + own_mate), :], ry.at[0], (down, j))
    back_mate = remote(p.at[mid, col(halo_mate), :], rxp, (i, mate))
    upper, lower = pl.ds(RAD, B - RAD), pl.ds(B, RAD)
    back_away = [remote(p.at[a, col(halo_away), :], rxo.at[b], (i, away))
                 for a, b in ((upper, pl.ds(0, B - RAD)), (lower, pl.ds(B - RAD, RAD)))]

    def halo_back(start, n):
        def step(g, c):
            x_backward(start + jnp.minimum(4 * g, RAD - 4), 4, n)
            return c

        lax.fori_loop(0, 4, step, 0, unroll=4)

    for c in (*relay_away, *pass_bottom):
        c.wait_recv()
    edge_rows(RAD + B, 2)
    y_forward_halo(list(range(RAD + B, ROWS)))
    load_rec.wait()
    lax.fori_loop(2, 4, depth, 0)
    y_backward([range(47, 55), range(55, 62)])
    halo_back(RAD + B, 2)
    sum_away.start()
    mate_bottom.start()
    for n in range(2):
        edge_down[n].wait_recv()
        pass_top[n].start()
    for c in (*corner_down, *relay_down, *pass_top):
        c.wait_recv()
    edge_rows(0, 1)
    y_forward_halo(list(range(0, RAD)))
    lax.fori_loop(0, 2, depth, 0)
    mate_bottom.wait_recv()
    p[bottom, col(H + own_mate), :] += rpc[1]
    back_down.start()
    y_backward([range(0, 8), range(8, 15)])
    halo_back(0, 1)
    sum_up.start()
    mate_top.start()
    sum_away.wait_recv()
    p[bottom, col(halo_away), :] += rq[...]
    sum_down.start()
    mate_top.wait_recv()
    p[top, col(H + own_mate), :] += rpc[0]
    back_up.start()
    sum_corner.start()

    y_backward([range(RAD + 8 * b, RAD + 8 * b + 8) for b in range(4)])

    def own_back(g, c):
        x_backward(RAD + 4 * g, 4, 0)
        return c

    lax.fori_loop(0, B // 4, own_back, 0)
    back_away[0].start()
    back_mate.start()
    sum_up.wait_recv()
    p[lower, col(halo_away), :] += rup[0]
    back_away[1].start()

    back_mate.wait_recv()
    p[mid, col(H + own_mate), :] += rxp[...]
    back_down.wait_recv()
    p[pl.ds(RAD, RAD), col(H + own_mate), :] += ry[0]
    back_up.wait_recv()
    p[lower, col(H + own_mate), :] += ry[1]
    sum_corner.wait_recv()
    p[lower, col(mine), :] += rup[1]
    sum_down.wait_recv()
    p[pl.ds(RAD, RAD), col(mine), :] += rdn[...]
    back_away[0].wait_recv()
    back_away[1].wait_recv()
    p[mid, col(mine), :] += rxo[...]
    own = (mid, pl.ds(H, B), slice(None))
    out[...] = u[own] * (p[own] * (1.0 / VIEWS))

    for c in (side_mate, *corner_up, *corner_down, *edge_up, *edge_down, *side_away, *relay_down, *relay_away,
              *pass_top, *pass_bottom, mate_bottom, mate_top, sum_away, sum_up, sum_corner, sum_down, back_up, back_down,
              back_mate, *back_away):
        c.wait_send()


def body(ny, nx, current, recorded, psf_depth, psf_rows, psf_cols):
    hbm = pl.BlockSpec(memory_space=pl.ANY)
    smem = pl.BlockSpec(memory_space=pltpu.SMEM)
    return pl.pallas_call(
        functools.partial(kernel, ny, nx),
        out_shape=jax.ShapeDtypeStruct((B, B, Z), F32),
        in_specs=[hbm, hbm, smem, smem, smem],
        out_specs=pl.BlockSpec(memory_space=pltpu.VMEM),
        scratch_shapes=[
            pltpu.VMEM((ROWS, COLS, Z), F32),
            pltpu.VMEM((ROWS, VIEWS * B, Z), F32),
            pltpu.VMEM((B, VIEWS * B, Z), F32),
            pltpu.VMEM((B, VIEWS * B, Z), F32),
            pltpu.VMEM((VIEWS, B, B, Z), F32),
            pltpu.VMEM((ROWS, COLS, Z), F32),
            pltpu.VMEM((2, RAD, H, Z), F32),
            pltpu.VMEM((B, H, Z), F32),
            pltpu.VMEM((B, H, Z), F32),
            pltpu.VMEM((2, RAD, H, Z), F32),
            pltpu.VMEM((RAD, H, Z), F32),
            pltpu.VMEM((RAD, H, Z), F32),
            pltpu.VMEM((2, RAD, H, Z), F32),
            pltpu.VMEM((3, VIEWS * B, 3 * COLS), BF16),
            pltpu.VMEM((HL, 3 * COLS), BF16),
            pltpu.VMEM((3, COLS, 3 * Z), BF16),
            pltpu.VMEM((VIEWS, 3 * Z, Z), BF16),
            pltpu.VMEM((VIEWS, 3 * Z, Z), BF16),
            pltpu.SemaphoreType.DMA((2,)),
            pltpu.SemaphoreType.DMA((32,)),
            pltpu.SemaphoreType.DMA((32,)),
        ],
        compiler_params=pltpu.CompilerParams(
            collective_id=0, has_side_effects=True, vmem_limit_bytes=60 * 1024 * 1024),
        name="richardson_lucy",
    )(current, recorded, psf_depth, psf_rows, psf_cols)


def solution(mesh):
    placed = (P("gy", "gx", None), P(None, "gy", "gx", None), P(), P(), P())
    return jax.shard_map(
        functools.partial(body, mesh.shape["gy"], mesh.shape["gx"]),
        mesh=mesh, in_specs=placed, out_specs=P("gy", "gx", None), check_vma=False
    )
```

```python
import functools

import jax
import jax.numpy as jnp
from jax import lax
from jax.experimental import pallas as pl
from jax.experimental.pallas import tpu as pltpu
from jax.sharding import PartitionSpec as P

F32 = jnp.float32
BF16 = jnp.bfloat16
TAPS = 31
RAD = 15
VIEWS = 4
B = 32
H = 16
HL = 64
ROWS = B + 2 * RAD
COLS = B + 2 * H
Z = 128


def split(x):
    hi = x.astype(BF16)
    return hi, (x - hi.astype(F32)).astype(BF16)


def triple_rows(x):
    hi, lo = split(x)
    return jnp.concatenate([hi, lo, hi], axis=0)


def triple_lanes(x):
    hi, lo = split(x)
    return jnp.concatenate([hi, lo, hi], axis=1)


def dot(a, b):
    return jnp.dot(a, b, preferred_element_type=F32)


def tap_sum(ref, v):
    total = ref[v, 0]
    for t in range(1, TAPS):
        total = total + ref[v, t]
    return total


def kernel(ny, nx, cur, rec, kz, ky, kx, out, u, xb, yb, gb, rv, p, ry, rxp, rxo, rup, rdn, rq, rpc,
           tf, tfm, tb, wf, wb, local_sem, send_sem, recv_sem):
    i = lax.axis_index("gy")
    j = lax.axis_index("gx")
    side = lax.rem(j, 2)
    up = lax.rem(i + ny - 1, ny)
    down = lax.rem(i + 1, ny)
    away = lax.rem(j + nx - 1 + 2 * side, nx)
    mate = j + 1 - 2 * side

    def col(x):
        return pl.ds(pl.multiple_of(x, H), H)

    own_away = H * side
    own_mate = H * (1 - side)
    halo_away = 48 * side
    halo_mate = 48 * (1 - side)

    load_rec = pltpu.make_async_copy(rec, rv, local_sem.at[0])
    load_cur = pltpu.make_async_copy(cur, u.at[pl.ds(RAD, B), pl.ds(H, B), :], local_sem.at[1])
    load_cur.start()
    load_rec.start()

    barrier = pltpu.get_barrier_semaphore()
    peers = [(up, j), (down, j), (i, away), (i, mate), (up, away), (down, away)]
    for peer in peers:
        pl.semaphore_signal(barrier, inc=1, device_id=peer, device_id_type=pl.DeviceIdType.MESH)
    pl.semaphore_wait(barrier, len(peers))

    count = [0]

    def remote(src, dst, peer):
        k = count[0]
        count[0] += 1
        return pltpu.make_async_remote_copy(
            src_ref=src, dst_ref=dst, send_sem=send_sem.at[k], recv_sem=recv_sem.at[k],
            device_id=peer, device_id_type=pl.DeviceIdType.MESH)

    near_top, far_top = pl.ds(7, 8), pl.ds(0, 7)
    near_bottom, far_bottom = pl.ds(47, 8), pl.ds(55, 7)
    top, bottom, mid = pl.ds(0, RAD), pl.ds(RAD + B, RAD), pl.ds(RAD, B)
    to_top = ((pl.ds(24, 8), near_top), (pl.ds(17, 7), far_top))
    to_bottom = ((pl.ds(0, 8), near_bottom), (pl.ds(8, 7), far_bottom))
    mine = H + own_away
    theirs = 48 - mine
    side_mate = remote(cur.at[:, col(own_mate), :], u.at[mid, col(48 - halo_mate), :], (i, mate))

    def corner(rows, peer):
        return [remote(cur.at[a, col(own_away), :], u.at[b, col(48 - halo_away), :], (peer, away)) for a, b in rows]

    def edge(rows, peer):
        return [remote(cur.at[a, col(own_mate), :], u.at[b, col(H + own_mate), :], (peer, j)) for a, b in rows]

    corner_up, corner_down = corner(to_bottom, up), corner(to_top, down)
    edge_up, edge_down = edge(to_bottom, up), edge(to_top, down)
    side_away = [remote(cur.at[pl.ds(r, n), col(own_away), :], u.at[pl.ds(RAD + r, n), col(48 - halo_away), :], (i, away))
                 for r, n in ((24, 8), (17, 7), (0, 17))]
    relay_down = [remote(u.at[pl.ds(RAD + r, n), col(halo_away), :], u.at[b, col(theirs), :], (down, away))
                  for r, n, b in ((24, 8, near_top), (17, 7, far_top))]
    relay_away = [remote(u.at[b, col(halo_away), :], u.at[b, col(theirs), :], (i, away))
                  for b in (near_bottom, far_bottom)]
    pass_top = [remote(u.at[b, col(H + own_mate), :], u.at[b, col(48 - halo_mate), :], (i, mate))
                for b in (near_top, far_top)]
    pass_bottom = [remote(u.at[b, col(H + own_mate), :], u.at[b, col(48 - halo_mate), :], (i, mate))
                   for b in (near_bottom, far_bottom)]
    side_mate.start()
    corner_up[0].start()
    corner_up[1].start()
    side_away[0].start()
    side_away[1].start()
    side_away[2].start()
    edge_up[0].start()
    edge_up[1].start()

    row_id = lax.broadcasted_iota(jnp.int32, (H, Z), 0)
    lane_id = lax.broadcasted_iota(jnp.int32, (H, Z), 1)
    low = jnp.where(j == 0, H, 0)
    high = jnp.where(j == nx - 1, H + B, COLS)
    def column_bands(half, base):
        parts = []
        for v in range(VIEWS):
            band = jnp.zeros((H, Z), F32)
            for t in range(TAPS):
                band = jnp.where(lane_id - row_id == half - base + t + 1, kx[v, t], band)
            band = band / jnp.full((H, Z), tap_sum(kx, v), F32)
            parts.append(jnp.where((lane_id >= low - base) & (lane_id < high - base), band, 0.0))
        return jnp.concatenate(parts, axis=0)

    full = jnp.concatenate([column_bands(own_mate, 0), column_bands(own_away, 0)], axis=0)
    hi, lo = split(column_bands(own_mate, own_mate)[:, :COLS])
    tfm[:, 0:COLS] = hi
    tfm[:, COLS:2 * COLS] = hi
    tfm[:, 2 * COLS:3 * COLS] = lo
    flipped = full.T[:COLS]
    keep_top = jnp.where(i == 0, 0.0, 1.0).astype(F32)
    keep_bottom = jnp.where(i == ny - 1, 0.0, 1.0).astype(F32)
    for n, keep in enumerate((None, keep_top, keep_bottom)):
        a = full if keep is None else full * keep
        b = flipped if keep is None else flipped * keep
        hi, lo = split(a[:, :COLS])
        tf[n, :, 0:COLS] = hi
        tf[n, :, COLS:2 * COLS] = hi
        tf[n, :, 2 * COLS:3 * COLS] = lo
        hi, lo = split(b)
        tb[n, :, 0:Z] = hi
        tb[n, :, Z:2 * Z] = hi
        tb[n, :, 2 * Z:3 * Z] = lo

    def depth_matrix(v, c):
        r = lax.broadcasted_iota(jnp.int32, (Z, Z), 0)
        l = lax.broadcasted_iota(jnp.int32, (Z, Z), 1)
        band = jnp.zeros((Z, Z), F32)
        for t in range(TAPS):
            band = jnp.where(r - l == t - RAD, kz[v, t], band)
        band = band / jnp.full((Z, Z), tap_sum(kz, v) * tap_sum(ky, v), F32)
        for ref, m in ((wf, band), (wb, band.T)):
            hi, lo = split(m)
            ref[v, 0:Z, :] = hi
            ref[v, Z:2 * Z, :] = hi
            ref[v, 2 * Z:3 * Z, :] = lo
        return c

    lax.fori_loop(0, VIEWS, depth_matrix, 0)

    def x_forward(start, count, n, lines=(0, 2 * HL)):
        data = jnp.concatenate([triple_rows(u[start + r]) for r in range(count)], axis=1)
        res = dot(tf[n, lines[0]:lines[1]], data)
        for r in range(count):
            xb[start + r, lines[0]:lines[1]] = res[:, r * Z:(r + 1) * Z]

    def mate_rows():
        def step(g, c):
            reach = pl.ds(pl.multiple_of(own_mate, H), 3 * H)
            none = jnp.zeros((H, Z), F32)
            data = jnp.concatenate(
                [triple_rows(jnp.concatenate([u[RAD + 4 * g + r, reach, :], none], axis=0)) for r in range(4)], axis=1)
            res = dot(tfm[...], data)
            for r in range(4):
                xb[RAD + 4 * g + r, 0:HL] = res[:, r * Z:(r + 1) * Z]
            return c

        lax.fori_loop(0, B // 4, step, 0)

    def own_rows(lines):
        def step(g, c):
            x_forward(RAD + 4 * g, 4, 0, lines)
            return c

        lax.fori_loop(0, B // 4, step, 0)

    def y_forward_own(n, c):
        off = pl.ds(pl.multiple_of(n * 8, 8), 8)
        v = lax.rem(n // 2, VIEWS)
        w = [ky[v, t] for t in range(TAPS)]
        for b in range(4):
            acc = [None] * 8
            for r in range(max(RAD, 8 * b), min(RAD + B - 1, 8 * b + 37) + 1):
                x = xb[r, off, :]
                for o in range(8):
                    t = r - (8 * b + o)
                    if 0 <= t < TAPS:
                        term = w[t] * x
                        acc[o] = term if acc[o] is None else acc[o] + term
            for o in range(8):
                yb[8 * b + o, off, :] = acc[o]
        return c

    load_cur.wait()
    side_mate.wait_recv()
    mate_rows()
    lax.fori_loop(0, 8, y_forward_own, 0)
    corner_up[0].wait_recv()
    corner_up[1].wait_recv()
    relay_away[0].start()
    relay_away[1].start()
    corner_down[0].start()
    corner_down[1].start()
    side_away[0].wait_recv()
    relay_down[0].start()
    side_away[1].wait_recv()
    relay_down[1].start()
    side_away[2].wait_recv()
    edge_down[0].start()
    edge_down[1].start()
    own_rows((HL, 2 * HL))
    lax.fori_loop(8, 16, y_forward_own, 0)
    edge_up[0].wait_recv()
    pass_bottom[0].start()
    edge_up[1].wait_recv()
    pass_bottom[1].start()

    def y_forward_halo(rows):
        def step(n, c):
            off = pl.ds(pl.multiple_of(n * 8, 8), 8)
            v = lax.rem(n // 2, VIEWS)
            w = [ky[v, t] for t in range(TAPS)]
            for b in range(4):
                outs = [8 * b + o for o in range(8)]
                acc = {}
                for r in rows:
                    hits = [o for o in outs if 0 <= r - o < TAPS]
                    if not hits:
                        continue
                    x = xb[r, off, :]
                    for o in hits:
                        term = w[r - o] * x
                        acc[o] = acc[o] + term if o in acc else term
                for o, a in acc.items():
                    yb[o, off, :] += a
            return c

        lax.fori_loop(0, 16, step, 0, unroll=2)

    def depth(n, c):
        rows = pl.ds(pl.multiple_of(n * 8, 8), 8)
        lines = [[pl.ds(h * HL + v * H, H) for h in range(2)] for v in range(VIEWS)]
        halves = (col(own_mate), col(own_away))

        def flat(x, y):
            return jnp.concatenate([x.reshape(8 * H, Z), y.reshape(8 * H, Z)], axis=0)

        data = [triple_lanes(flat(*(yb[rows, q, :] for q in lines[v]))) for v in range(VIEWS)]
        blurred = [dot(data[v], wf[v]) for v in range(VIEWS)]
        images = [flat(*(rv[v, rows, q, :] for q in halves)) for v in range(VIEWS)]
        data = [triple_lanes(images[v] / blurred[v]) for v in range(VIEWS)]
        res = [dot(data[v], wb[v]) for v in range(VIEWS)]
        for v in range(VIEWS):
            for h in range(2):
                gb[rows, lines[v][h], :] = res[v][h * 8 * H:(h + 1) * 8 * H].reshape(8, H, Z)
        return c

    def edge_rows(start, n):
        for g in (0, 4, 8, RAD - 4):
            x_forward(start + g, 4, n)

    def y_backward(rows):
        def step(n, c):
            off = pl.ds(pl.multiple_of(n * 8, 8), 8)
            v = lax.rem(n // 2, VIEWS)
            w = [ky[v, t] for t in range(TAPS)]
            for group in rows:
                acc = {}
                for q in range(max(0, group[0] - TAPS + 1), min(B - 1, group[-1]) + 1):
                    x = gb[q, off, :]
                    for r in group:
                        if 0 <= r - q < TAPS:
                            term = w[r - q] * x
                            acc[r] = acc[r] + term if r in acc else term
                for r, a in acc.items():
                    xb[r, off, :] = a
            return c

        lax.fori_loop(0, 16, step, 0, unroll=2)

    def x_backward(start, count, n):
        data = jnp.concatenate([triple_rows(xb[start + r]) for r in range(count)], axis=1)
        res = dot(tb[n], data)
        for r in range(count):
            p[start + r] = res[:, r * Z:(r + 1) * Z]

    mate_bottom = remote(p.at[bottom, col(halo_mate), :], rpc.at[1], (i, mate))
    mate_top = remote(p.at[top, col(halo_mate), :], rpc.at[0], (i, mate))
    sum_away = remote(p.at[bottom, col(mine), :], rq, (i, away))
    sum_up = remote(p.at[top, col(mine), :], rup.at[0], (up, away))
    sum_corner = remote(p.at[top, col(halo_away), :], rup.at[1], (up, away))
    sum_down = remote(p.at[bottom, col(halo_away), :], rdn, (down, away))
    back_up = remote(p.at[top, col(H + own_mate), :], ry.at[1], (up, j))
    back_down = remote(p.at[bottom, col(H + own_mate), :], ry.at[0], (down, j))
    back_mate = remote(p.at[mid, col(halo_mate), :], rxp, (i, mate))
    upper, lower = pl.ds(RAD, B - RAD), pl.ds(B, RAD)
    back_away = [remote(p.at[a, col(halo_away), :], rxo.at[b], (i, away))
                 for a, b in ((upper, pl.ds(0, B - RAD)), (lower, pl.ds(B - RAD, RAD)))]

    def halo_back(start, n):
        def step(g, c):
            x_backward(start + jnp.minimum(4 * g, RAD - 4), 4, n)
            return c

        lax.fori_loop(0, 4, step, 0, unroll=4)

    for c in (*relay_away, *pass_bottom):
        c.wait_recv()
    edge_rows(RAD + B, 2)
    y_forward_halo(list(range(RAD + B, ROWS)))
    load_rec.wait()
    lax.fori_loop(2, 4, depth, 0)
    y_backward([range(47, 55), range(55, 62)])
    for n in range(2):
        edge_down[n].wait_recv()
        pass_top[n].start()
    halo_back(RAD + B, 2)
    sum_away.start()
    mate_bottom.start()
    for c in (*corner_down, *relay_down, *pass_top):
        c.wait_recv()
    edge_rows(0, 1)
    y_forward_halo(list(range(0, RAD)))
    lax.fori_loop(0, 2, depth, 0)
    mate_bottom.wait_recv()
    p[bottom, col(H + own_mate), :] += rpc[1]
    back_down.start()
    y_backward([range(0, 8), range(8, 15)])
    halo_back(0, 1)
    sum_up.start()
    mate_top.start()
    sum_away.wait_recv()
    p[bottom, col(halo_away), :] += rq[...]
    sum_down.start()
    mate_top.wait_recv()
    p[top, col(H + own_mate), :] += rpc[0]
    back_up.start()
    sum_corner.start()

    y_backward([range(RAD + 8 * b, RAD + 8 * b + 8) for b in range(4)])

    def own_back(g, c):
        x_backward(RAD + 4 * g, 4, 0)
        return c

    lax.fori_loop(0, B // 4, own_back, 0)
    back_away[0].start()
    back_mate.start()
    sum_up.wait_recv()
    p[lower, col(halo_away), :] += rup[0]
    back_away[1].start()

    back_mate.wait_recv()
    p[mid, col(H + own_mate), :] += rxp[...]
    back_down.wait_recv()
    p[pl.ds(RAD, RAD), col(H + own_mate), :] += ry[0]
    back_up.wait_recv()
    p[lower, col(H + own_mate), :] += ry[1]
    sum_corner.wait_recv()
    p[lower, col(mine), :] += rup[1]
    sum_down.wait_recv()
    p[pl.ds(RAD, RAD), col(mine), :] += rdn[...]
    back_away[0].wait_recv()
    back_away[1].wait_recv()
    p[mid, col(mine), :] += rxo[...]
    own = (mid, pl.ds(H, B), slice(None))
    out[...] = u[own] * (p[own] * (1.0 / VIEWS))

    for c in (side_mate, *corner_up, *corner_down, *edge_up, *edge_down, *side_away, *relay_down, *relay_away,
              *pass_top, *pass_bottom, mate_bottom, mate_top, sum_away, sum_up, sum_corner, sum_down, back_up, back_down,
              back_mate, *back_away):
        c.wait_send()


def body(ny, nx, current, recorded, psf_depth, psf_rows, psf_cols):
    hbm = pl.BlockSpec(memory_space=pl.ANY)
    smem = pl.BlockSpec(memory_space=pltpu.SMEM)
    return pl.pallas_call(
        functools.partial(kernel, ny, nx),
        out_shape=jax.ShapeDtypeStruct((B, B, Z), F32),
        in_specs=[hbm, hbm, smem, smem, smem],
        out_specs=pl.BlockSpec(memory_space=pltpu.VMEM),
        scratch_shapes=[
            pltpu.VMEM((ROWS, COLS, Z), F32),
            pltpu.VMEM((ROWS, VIEWS * B, Z), F32),
            pltpu.VMEM((B, VIEWS * B, Z), F32),
            pltpu.VMEM((B, VIEWS * B, Z), F32),
            pltpu.VMEM((VIEWS, B, B, Z), F32),
            pltpu.VMEM((ROWS, COLS, Z), F32),
            pltpu.VMEM((2, RAD, H, Z), F32),
            pltpu.VMEM((B, H, Z), F32),
            pltpu.VMEM((B, H, Z), F32),
            pltpu.VMEM((2, RAD, H, Z), F32),
            pltpu.VMEM((RAD, H, Z), F32),
            pltpu.VMEM((RAD, H, Z), F32),
            pltpu.VMEM((2, RAD, H, Z), F32),
            pltpu.VMEM((3, VIEWS * B, 3 * COLS), BF16),
            pltpu.VMEM((HL, 3 * COLS), BF16),
            pltpu.VMEM((3, COLS, 3 * Z), BF16),
            pltpu.VMEM((VIEWS, 3 * Z, Z), BF16),
            pltpu.VMEM((VIEWS, 3 * Z, Z), BF16),
            pltpu.SemaphoreType.DMA((2,)),
            pltpu.SemaphoreType.DMA((32,)),
            pltpu.SemaphoreType.DMA((32,)),
        ],
        compiler_params=pltpu.CompilerParams(
            collective_id=0, has_side_effects=True, vmem_limit_bytes=60 * 1024 * 1024),
        name="richardson_lucy",
    )(current, recorded, psf_depth, psf_rows, psf_cols)


def solution(mesh):
    placed = (P("gy", "gx", None), P(None, "gy", "gx", None), P(), P(), P())
    return jax.shard_map(
        functools.partial(body, mesh.shape["gy"], mesh.shape["gx"]),
        mesh=mesh, in_specs=placed, out_specs=P("gy", "gx", None), check_vma=False
    )
```
